512 devices in a mesh: mesh: 64 (over y, z), mem: 8 (over x, core).
Axes of the slice: x: 4, y: 4, z: 16, core: 2. Of those that a mesh axis runs over, the one named last changes fastest.
Arguments:
- ensemble: bfloat16 [40, 240, 24576], P('mem', None, 'mesh'), may hold values from -6 to 6
- ovl_owner: int32 [1536, 2], P('mesh'), may hold values from 0 to 63, all different within a row; in each aligned block of 24 rows (0 to 23, 24 to 47, ...) at most 2 rows name the same one
- ovl_patch: int32 [1536, 2], P('mesh'), may hold values from 0 to 7
- ovl_weight: bfloat16 [1536, 2, 16, 8], P('mesh'), may hold values from 0.0099487305 to 0.19921875
- letkf_weight: float32 [64, 40, 40], P('mesh'), may hold values from -1 to 1
Outputs:
- analysis: bfloat16 [40, 240, 24576], P('mem', None, 'mesh')
The draws below stay inside these ranges and needn't reach their ends.
Inputs may be any that keep to these rules, and one draw needn't show every extreme that they name: `ovl_owner`: within the 24 rows of one mesh index, the two entries of a row differ, and each owner is named at most 2 times; some owner exactly 2 times.
All inputs are finite; a program needn't handle non-finite values.
Results may differ from the reference program's by a relative error of at most 0.0015.
Values may be sent and summed in bfloat16 or wider, within the bound.
No kernel may reach another device: no remote copies, remote signals or barrier semaphores. Data moves between devices by JAX's collectives and lax.ppermute only.
A program may use at most 128 MiB of HBM per device.

```python
import math
import jax
import jax.numpy as jnp
import numpy as np
from jax import lax

M = 40
C = 240
BE = 16
PG = 8
PATCH_TILE = 8
NBLK = 24
NPATCH_DEV = 8
CAP = 2
ELEMS = 24576
BLOCKS = 1536
TILES = 64
N_MESH = 64


def touch_ends(entries, stream_key, low, top_value):
    dims = entries.shape
    place = [jax.random.randint(jax.random.fold_in(stream_key, axis), (), 0, dims[axis]) for axis in range(len(dims))]
    entries = entries.at[tuple(place)].set(low)
    longest = dims.index(max(dims))
    place[longest] = (place[longest] + 1) % dims[longest]
    return entries.at[tuple(place)].set(top_value)


def levels(own_key, dims, cuts, least, top_value):
    level = 1.0
    for position, shards_of in cuts:
        draws = jax.random.uniform(jax.random.fold_in(jax.random.fold_in(own_key, 6), position), (shards_of,), jnp.float32, least / len(cuts), top_value / len(cuts))
        level = level * jnp.repeat(jnp.exp(draws), dims[position] // shards_of).reshape((-1,) + (1,) * (len(dims) - 1 - position))
    return level


def routed_block(stream_key, own, number, rows, number_of, top, most, lean):
    ranking = jax.random.permutation(stream_key, number_of)
    heavy_load, usual = load_shares(number_of, rows * top, most, lean, True), load_shares(number_of, rows * top, most, lean, False)
    places = jnp.arange(number_of)

    def named(sizes, rotation):
        used = int((sizes > 0).sum())
        fixed = max(1, used // 4)
        passed = fixed + (places - fixed + rotation * (used - fixed)) % max(1, number_of - fixed)
        return jnp.zeros((number_of,), jnp.int32).at[ranking[jnp.where(places < fixed, places, passed)]].set(jnp.asarray(sizes, jnp.int32))

    sizes = jnp.where(number % 4 == 0, named(heavy_load, number // 4), named(usual, number - number // 4 - 1))
    mixed = jax.random.permutation(jax.random.fold_in(own, 3), number_of)
    source_of, sink = mixed[0:number_of // 2 * 2:2], mixed[1:number_of // 2 * 2:2]
    room = jnp.minimum(sizes[source_of] - 1, most - sizes[sink]) // 2
    room = jnp.where((source_of == ranking[0]) | (sink == ranking[0]) | (sizes[sink] == 0), 0, jnp.maximum(room, 0))
    passed = jax.random.randint(jax.random.fold_in(own, 4), (number_of // 2,), 0, 1 << 20) % (room + 1)
    sizes = sizes.at[source_of].add(-passed).at[sink].add(passed)
    items = jnp.searchsorted(jnp.cumsum(sizes), jnp.arange(rows * top), side="right").astype(jnp.int32)
    grid = items.reshape(top, rows).T
    grid = grid[jax.random.permutation(jax.random.fold_in(own, 1), rows)]
    rotation = jax.random.randint(jax.random.fold_in(own, 2), (rows, 1), 0, top)
    return jnp.take_along_axis(grid, (jnp.arange(top)[None, :] + rotation) % top, axis=1)


def load_shares(amount, total, limit, slope, full):
    loads = [(1 << 20) // math.isqrt(rank ** slope) + 1 for rank in range(1, amount + 1)]
    largest = limit if full else min(limit, max(-(-total // amount), total * loads[0] // sum(loads)))
    least = 1 if total - largest >= amount - 1 else 0
    given, rest = [largest] + [least] * (amount - 1), total - largest - least * (amount - 1)
    while rest > 0:
        free = [i for i in range(1, amount) if given[i] < largest] or [i for i in range(1, amount) if given[i] < limit]
        pool, remaining = sum([loads[i] for i in free]), rest
        for i in free:
            addition = min(limit - given[i], max(1, remaining * loads[i] // pool), rest)
            given[i] = given[i] + addition
            rest = rest - addition
    return np.array(given)


def scatter_about(own_key, dims, scale, limit, split=(), held_as=jnp.bfloat16):
    loudness = levels(own_key, dims, split, -0.22, 0.18) if split else 1.0
    entries = jax.random.normal(own_key, dims, jnp.float32) * scale * loudness
    return jnp.minimum(jnp.maximum(entries, -limit), limit).astype(held_as)


def setup_inputs(seed: int = 0) -> dict:
    streams_of = jax.random.split(jax.random.key(seed), 6)
    ensemble = scatter_about(streams_of[0], (M, C, ELEMS), 1.0, 6.0, ((0, 8), (2, 64)))
    ovl_owner_keys = jax.random.split(jax.random.fold_in(streams_of[1], 1), BLOCKS // NBLK)
    ovl_owner_turns = jax.random.permutation(jax.random.fold_in(streams_of[1], 3), BLOCKS // NBLK)
    ovl_owner = jax.vmap(lambda own, number: routed_block(jax.random.fold_in(streams_of[1], 2), own, number, NBLK, N_MESH, 2, CAP, 2))(ovl_owner_keys, ovl_owner_turns).reshape((BLOCKS, 2))
    ovl_patch = touch_ends(jax.random.randint(streams_of[2], (BLOCKS, 2), 0, NPATCH_DEV), jax.random.fold_in(streams_of[2], 1), 0, NPATCH_DEV - 1).astype(jnp.int32)
    ovl_weight = jnp.clip(jnp.exp(math.log(0.19921875) - 2.9969585 * jax.random.uniform(streams_of[3], (BLOCKS, 2, BE, PG), jnp.float32) ** levels(streams_of[3], (BLOCKS, 2, BE, PG), ((0, 64),), -0.2, 0.2)), 0.0099487305, 0.19921875).astype(jnp.bfloat16)
    letkf_weight = scatter_about(streams_of[4], (TILES, M, M), M ** -0.5, 1.0, ((0, 64),), jnp.float32)
    return {"ensemble": ensemble, "ovl_owner": ovl_owner, "ovl_patch": ovl_patch, "ovl_weight": ovl_weight, "letkf_weight": letkf_weight}


def reference(ensemble, ovl_owner, ovl_patch, ovl_weight, letkf_weight):
    patch_total = N_MESH * NPATCH_DEV
    destination = (ovl_owner * NPATCH_DEV + ovl_patch).astype(jnp.int32)
    blocks_x = ensemble.reshape(M, C, N_MESH, NBLK, BE)

    def forward(carry, device):
        patch_sums, coverage = carry
        device_blocks = lax.dynamic_index_in_dim(blocks_x, device, 2, keepdims=False)
        device_margin = lax.dynamic_slice_in_dim(ovl_weight, device * NBLK, NBLK, 0)
        device_dest = lax.dynamic_slice_in_dim(destination, device * NBLK, NBLK, 0).reshape(-1)
        pieces = jnp.einsum('mcbe,bkeg->bkmcg', device_blocks.astype(jnp.float32), device_margin.astype(jnp.float32)).astype(jnp.bfloat16)
        patch_sums = patch_sums.at[device_dest].add(pieces.reshape(-1, M, C, PG).astype(jnp.float32))
        column_sums = jnp.sum(device_margin.astype(jnp.float32), axis=2).reshape(-1, PG)
        coverage = coverage.at[device_dest].add(column_sums)
        return (patch_sums, coverage), None

    start_sums = jnp.zeros((patch_total, M, C, PG), jnp.float32)
    start_cover = jnp.zeros((patch_total, PG), jnp.float32)
    devices = jnp.arange(N_MESH, dtype=jnp.int32)
    (patch_sums, coverage), _ = lax.scan(forward, (start_sums, start_cover), devices)
    grid_field = (patch_sums / jnp.maximum(coverage, 1.0)[:, None, None, :]).astype(jnp.bfloat16)
    tile_view = grid_field.reshape(TILES, PATCH_TILE, M, C, PG).astype(jnp.float32)
    mixed = jnp.einsum('tjmcg,tmn->tjncg', tile_view, letkf_weight, precision=lax.Precision.HIGHEST)
    increment = (mixed - tile_view).astype(jnp.bfloat16).reshape(patch_total, M, C, PG)

    def backward(carry, device):
        device_blocks = lax.dynamic_index_in_dim(blocks_x, device, 2, keepdims=False)
        device_margin = lax.dynamic_slice_in_dim(ovl_weight, device * NBLK, NBLK, 0).astype(jnp.float32)
        device_dest = lax.dynamic_slice_in_dim(destination, device * NBLK, NBLK, 0).reshape(-1)
        gathered = jnp.take(increment, device_dest, axis=0).reshape(NBLK, 2, M, C, PG)
        element_area = jnp.sum(device_margin, axis=(1, 3))
        correction = jnp.einsum('bkmcg,bkeg->mcbe', gathered.astype(jnp.float32), device_margin) / element_area[None, None]
        updated = (device_blocks.astype(jnp.float32) + correction).astype(jnp.bfloat16)
        return carry, updated

    _, stacked = lax.scan(backward, jnp.zeros((), jnp.float32), devices)
    return jnp.transpose(stacked, (1, 2, 0, 3, 4)).reshape(M, C, N_MESH * NBLK * BE)
```

```python
import jax
import jax.numpy as jnp
from jax import lax
from jax.experimental import pallas as pl
from jax.experimental.pallas import tpu as pltpu
from jax.sharding import PartitionSpec as P

MESH = 64
MEM = 8
MEMBERS = 5
CHANNELS = 240
ELEMENTS = 384
CELLS = 8
PATCHES = 512
ROWS = 16
THIRDS = 3
WIDTH = 512
SIDE = 96
COLUMNS = 160
BF = jnp.bfloat16
F32 = jnp.float32
VMEM_BYTES = 40 * 1024 * 1024


def iota(shape, dim):
    return lax.broadcasted_iota(jnp.int32, shape, dim)


def dot(a, b):
    return jnp.dot(a, b, preferred_element_type=F32)


def dot_nt(a, b):
    return lax.dot_general(a, b, (((1,), (1,)), ((), ())), preferred_element_type=F32)


def one_hot(mask):
    return jnp.where(mask, 1.0, 0.0).astype(BF)


def member_tiles(group):
    return [(half, m, group * 32 + half * 16) for half in range(2) for m in range(MEMBERS)]


def source_kernel(mem_ref, ens_ref, margin_ref, owner_ref, patch_ref, letkf_ref, out_ref, spread_ref):
    lane24 = iota((24, ELEMENTS), 1)
    block_of = (lane24 // 128) * 8 + lane24 % 8
    pick_block = iota((24, ELEMENTS), 0) == block_of
    expanded = dot(margin_ref[...], one_hot(pick_block))
    row = iota((256, ELEMENTS), 0)
    lane = iota((256, ELEMENTS), 1)
    fits = (row // 128 == (lane % 16) // 8) & (row % 8 == (lane % 128) // 16)
    expanded = jnp.where(fits, expanded, 0.0).astype(BF)
    fold = one_hot((iota((ELEMENTS, 256), 1) % 128) // 8 == iota((ELEMENTS, 256), 0) % 16)
    spread = dot(fold, expanded)
    er = iota((ELEMENTS, ELEMENTS), 0)
    el = iota((ELEMENTS, ELEMENTS), 1)
    spread = jnp.where(er // 16 == (el // 128) * 8 + el % 8, spread, 0.0)
    sums = jnp.sum(spread, axis=0, keepdims=True)
    spread = spread.astype(BF)
    spread_ref[...] = spread
    high = sums.astype(BF).astype(F32)
    low = sums - high

    dest = owner_ref[...] * 8 + patch_ref[...] - 256
    dest = dest.astype(F32).astype(BF)
    place = dot(dest, one_hot(pick_block))
    lane2 = iota((2, ELEMENTS), 1)
    place = jnp.sum(jnp.where((lane2 % 16) // 8 == iota((2, ELEMENTS), 0), place, 0.0), axis=0, keepdims=True)

    own = mem_ref[0] * MEMBERS
    pick_own = one_hot((iota((16, 40), 1) == own + iota((16, 40), 0) // 3) & (iota((16, 40), 0) < 15))
    mine = dot_nt(pick_own, letkf_ref[...].astype(BF))
    keep = (iota((16, 40), 1) // 16) == iota((16, 40), 0) % 3
    mine = jnp.where(keep, mine, 0.0).astype(BF)
    weights = dot(mine, one_hot(iota((40, 128), 0) % 16 == iota((40, 128), 1) % 16))

    def parts(value):
        return [value[:, 128 * h : 128 * h + 128] for h in range(THIRDS)]

    side = jnp.concatenate(
        parts(place) + parts(high) + parts(low) + [jnp.zeros((7, 128), F32), weights], axis=0
    )

    for group in range(8):
        tiles = []
        for half, m, start in member_tiles(group):
            if start < CHANNELS:
                tiles.append(ens_ref[m, start : start + 16, :])
            else:
                tiles.append(jnp.zeros((16, ELEMENTS), BF))
        pieces = dot(jnp.concatenate(tiles, axis=0), spread)
        for h in range(THIRDS):
            block = pieces[0:128, 128 * h : 128 * h + 128].T.astype(BF)
            out_ref[8 * group : 8 * group + 8, :, 128 * h : 128 * h + 128] = block.reshape(8, ROWS, 128)
        rest = jnp.concatenate(parts(pieces[128:160]) + [side], axis=0)
        out_ref[8 * group : 8 * group + 8, :, 384:512] = rest.T.astype(BF).reshape(8, ROWS, 128)


def hits(side, h):
    place = side[:, SIDE + h : SIDE + h + 1].astype(F32) + 256.0
    lanes = iota((MESH * ROWS, PATCHES), 1).astype(F32)
    return one_hot(lanes == place)


def patch_kernel(got_ref, out_ref, weight_ref):
    got = got_ref[...].reshape(MESH * ROWS, WIDTH)
    last = got[:, 384:512].astype(F32)
    last_t = last.T.astype(BF)
    total = jnp.zeros((128, PATCHES), F32)
    rest = jnp.zeros((32, PATCHES), F32)
    cover = jnp.zeros((1, PATCHES), F32)
    for h in range(THIRDS):
        first_t = got[:, 128 * h : 128 * h + 128].astype(F32).T.astype(BF)
        left = jnp.concatenate([first_t, last_t[32 * h : 32 * h + 32], last_t[96:112]], axis=0)
        sums = dot(left, hits(last, h))
        total = total + sums[0:128]
        rest = rest + sums[128:160]
        cover = cover + sums[163 + h : 164 + h] + sums[166 + h : 167 + h]
    cover = jnp.maximum(cover, 1.0)
    total = (total / cover).astype(BF)
    rest = (rest / cover).astype(BF)
    for q in range(MEM):
        out_ref[q, 0:128, :] = total
        out_ref[q, 128:160, :] = rest

    wide = last_t[112:128]
    lane = iota((ROWS, MESH * ROWS), 1)
    rows = jnp.concatenate(
        [jnp.where(lane % 16 == r, wide, jnp.zeros_like(wide)) for r in range(ROWS)], axis=0
    )
    tile = one_hot(
        iota((MESH * ROWS, PATCHES), 0) // 16 == iota((MESH * ROWS, PATCHES), 1) // 8
    )
    weight_ref[...] = dot(rows, tile)


def mixing_kernel(grid_ref, own_ref, weight_ref, got_ref, out_ref, inc_ref):
    for half in range(2):
        for lanes in range(PATCHES // 128):
            at = slice(128 * lanes, 128 * lanes + 128)
            mixed = [jnp.zeros((16, 128), F32) for _ in range(MEMBERS)]
            for m in range(MEM * MEMBERS):
                row = (half * MEMBERS + m % MEMBERS) * 16
                field = grid_ref[m // MEMBERS, row : row + 16, at].astype(F32)
                for n in range(MEMBERS):
                    w = (m % 16) * 16 + n * 3 + m // 16
                    mixed[n] = mixed[n] + weight_ref[w : w + 1, at] * field
            for n in range(MEMBERS):
                row = (half * MEMBERS + n) * 16
                inc_ref[row : row + 16, at] = mixed[n] - own_ref[0, row : row + 16, at].astype(F32)
    side = got_ref[...].reshape(MESH * ROWS, 128).astype(F32)
    first = inc_ref[0:128, :].T.astype(BF)
    small = inc_ref[128:160, :]
    last = jnp.zeros((MESH * ROWS, 128), F32)
    for h in range(THIRDS):
        pad = [jnp.zeros((32, PATCHES), F32)] * 4
        pad[h] = small
        right = jnp.concatenate([first, jnp.concatenate(pad, axis=0).T.astype(BF)], axis=1)
        back = dot(hits(side, h), right)
        out_ref[:, :, 128 * h : 128 * h + 128] = back[:, 0:128].astype(BF).reshape(MESH, ROWS, 128)
        last = last + back[:, 128:256]
    out_ref[:, :, 384:512] = last.astype(BF).reshape(MESH, ROWS, 128)


def final_kernel(back_ref, ens_ref, spread_ref, out_ref):
    spread = spread_ref[...]
    area = dot_nt(jnp.ones((16, ELEMENTS), BF), spread)[0:1]
    scale = 1.0 / area
    for group in range(8):
        def turned(k):
            block = back_ref[8 * group : 8 * group + 8, :, 128 * k : 128 * k + 128]
            return block.reshape(128, 128).astype(F32).T

        first = jnp.concatenate([turned(h) for h in range(THIRDS)], axis=1)
        last = turned(3)
        last = jnp.concatenate([last[32 * h : 32 * h + 32] for h in range(THIRDS)], axis=1)
        left = jnp.concatenate([first, last], axis=0).astype(BF)
        correction = dot_nt(left, spread) * scale
        for k, (half, m, start) in enumerate(member_tiles(group)):
            if start < CHANNELS:
                value = ens_ref[m, start : start + 16, :].astype(F32) + correction[16 * k : 16 * k + 16]
                out_ref[m, start : start + 16, :] = value.astype(BF)


def vmem():
    return pl.BlockSpec(memory_space=pltpu.VMEM)


def call(kernel, outs, ins, scratch=()):
    return pl.pallas_call(
        kernel,
        out_shape=[jax.ShapeDtypeStruct(s, d) for s, d in outs],
        in_specs=ins,
        out_specs=[vmem() for _ in outs],
        scratch_shapes=list(scratch),
        compiler_params=pltpu.CompilerParams(vmem_limit_bytes=VMEM_BYTES),
    )


def shards(ensemble, ovl_owner, ovl_patch, ovl_weight, letkf_weight):
    margin = ovl_weight.transpose(1, 2, 3, 0).reshape(256, 24)
    mem = lax.axis_index("mem").astype(jnp.int32).reshape(1)
    send, spread = call(
        source_kernel,
        [((MESH, ROWS, WIDTH), BF), ((ELEMENTS, ELEMENTS), BF)],
        [pl.BlockSpec(memory_space=pltpu.SMEM)] + [vmem()] * 5,
    )(mem, ensemble, margin, ovl_owner.T, ovl_patch.T, letkf_weight[0])
    got = lax.all_to_all(send, "mesh", split_axis=0, concat_axis=0, tiled=True)
    copies, weight = call(
        patch_kernel, [((MEM, COLUMNS, PATCHES), BF), ((256, PATCHES), F32)], [vmem()]
    )(got)
    grid = lax.all_to_all(copies, "mem", split_axis=0, concat_axis=0, tiled=True)
    (back,) = call(
        mixing_kernel,
        [((MESH, ROWS, WIDTH), BF)],
        [vmem()] * 4,
        [pltpu.VMEM((COLUMNS, PATCHES), F32)],
    )(grid, copies[0:1], weight, got[:, :, 384:512])
    returned = lax.all_to_all(back, "mesh", split_axis=0, concat_axis=0, tiled=True)
    (analysis,) = call(final_kernel, [((MEMBERS, CHANNELS, ELEMENTS), BF)], [vmem()] * 3)(
        returned, ensemble, spread
    )
    return analysis


def solution(mesh):
    in_specs = (
        P("mem", None, "mesh"),
        P("mesh", None),
        P("mesh", None),
        P("mesh", None, None, None),
        P("mesh", None, None),
    )
    out_specs = P("mem", None, "mesh")
    return jax.shard_map(shards, mesh=mesh, in_specs=in_specs, out_specs=out_specs, check_vma=False)
```

```python
import jax
import jax.numpy as jnp
from jax import lax
from jax.experimental import pallas as pl
from jax.experimental.pallas import tpu as pltpu
from jax.sharding import PartitionSpec as P

MESH = 64
MEM = 8
MEMBERS = 5
CHANNELS = 240
ELEMENTS = 384
CELLS = 8
PATCHES = 512
ROWS = 16
THIRDS = 3
WIDTH = 512
SIDE = 96
COLUMNS = 160
BF = jnp.bfloat16
F32 = jnp.float32
VMEM_BYTES = 40 * 1024 * 1024
SOURCE_VMEM_BYTES = 60 * 1024 * 1024


def iota(shape, dim):
    return lax.broadcasted_iota(jnp.int32, shape, dim)


def dot(a, b):
    return jnp.dot(a, b, preferred_element_type=F32)


def dot_nt(a, b):
    return lax.dot_general(a, b, (((1,), (1,)), ((), ())), preferred_element_type=F32)


def one_hot(mask):
    return jnp.where(mask, 1.0, 0.0).astype(BF)


def member_tiles(group):
    return [(half, m, group * 32 + half * 16) for half in range(2) for m in range(MEMBERS)]


def source_kernel(mem_ref, *refs):
    sources, (out_ref, spread_ref), landed, sems = refs[:5], refs[5:7], refs[7:12], refs[12]
    copies = [pltpu.make_async_copy(a, b, sems.at[k]) for k, (a, b) in enumerate(zip(sources, landed))]
    for copy in copies:
        copy.start()
    for copy in copies[1:]:
        copy.wait()
    ens_ref, margin_ref, owner_ref, patch_ref, letkf_ref = landed
    lane24 = iota((24, ELEMENTS), 1)
    block_of = (lane24 // 128) * 8 + lane24 % 8
    pick_block = iota((24, ELEMENTS), 0) == block_of
    expanded = dot(margin_ref[...], one_hot(pick_block))
    row = iota((256, ELEMENTS), 0)
    lane = iota((256, ELEMENTS), 1)
    fits = (row // 128 == (lane % 16) // 8) & (row % 8 == (lane % 128) // 16)
    expanded = jnp.where(fits, expanded, 0.0).astype(BF)
    fold = one_hot((iota((ELEMENTS, 256), 1) % 128) // 8 == iota((ELEMENTS, 256), 0) % 16)
    spread = dot(fold, expanded)
    er = iota((ELEMENTS, ELEMENTS), 0)
    el = iota((ELEMENTS, ELEMENTS), 1)
    spread = jnp.where(er // 16 == (el // 128) * 8 + el % 8, spread, 0.0)
    sums = jnp.sum(spread, axis=0, keepdims=True)
    spread = spread.astype(BF)
    spread_ref[...] = spread
    high = sums.astype(BF).astype(F32)
    low = sums - high

    dest = owner_ref[...] * 8 + patch_ref[...] - 256
    dest = dest.astype(F32).astype(BF)
    place = dot(dest, one_hot(pick_block))
    lane2 = iota((2, ELEMENTS), 1)
    place = jnp.sum(jnp.where((lane2 % 16) // 8 == iota((2, ELEMENTS), 0), place, 0.0), axis=0, keepdims=True)

    own = mem_ref[0] * MEMBERS
    pick_own = one_hot((iota((16, 40), 1) == own + iota((16, 40), 0) // 3) & (iota((16, 40), 0) < 15))
    mine = dot_nt(pick_own, letkf_ref[...].astype(BF))
    keep = (iota((16, 40), 1) // 16) == iota((16, 40), 0) % 3
    mine = jnp.where(keep, mine, 0.0).astype(BF)
    weights = dot(mine, one_hot(iota((40, 128), 0) % 16 == iota((40, 128), 1) % 16))

    def parts(value):
        return [value[:, 128 * h : 128 * h + 128] for h in range(THIRDS)]

    side = jnp.concatenate(
        parts(place) + parts(high) + parts(low) + [jnp.zeros((7, 128), F32), weights], axis=0
    )

    copies[0].wait()
    for group in range(8):
        tiles = []
        for half, m, start in member_tiles(group):
            if start < CHANNELS:
                tiles.append(ens_ref[m, start : start + 16, :])
            else:
                tiles.append(jnp.zeros((16, ELEMENTS), BF))
        pieces = dot(jnp.concatenate(tiles, axis=0), spread)
        for h in range(THIRDS):
            block = pieces[0:128, 128 * h : 128 * h + 128].T.astype(BF)
            out_ref[8 * group : 8 * group + 8, :, 128 * h : 128 * h + 128] = block.reshape(8, ROWS, 128)
        rest = jnp.concatenate(parts(pieces[128:160]) + [side], axis=0)
        out_ref[8 * group : 8 * group + 8, :, 384:512] = rest.T.astype(BF).reshape(8, ROWS, 128)


def hits(side, h):
    place = side[:, SIDE + h : SIDE + h + 1].astype(F32) + 256.0
    lanes = iota((MESH * ROWS, PATCHES), 1).astype(F32)
    return one_hot(lanes == place)


def patch_kernel(got_ref, out_ref, weight_ref):
    got = got_ref[...].reshape(MESH * ROWS, WIDTH)
    last = got[:, 384:512].astype(F32)
    last_t = last.T.astype(BF)
    total = jnp.zeros((128, PATCHES), F32)
    rest = jnp.zeros((32, PATCHES), F32)
    cover = jnp.zeros((1, PATCHES), F32)
    for h in range(THIRDS):
        first_t = got[:, 128 * h : 128 * h + 128].astype(F32).T.astype(BF)
        left = jnp.concatenate([first_t, last_t[32 * h : 32 * h + 32], last_t[96:112]], axis=0)
        sums = dot(left, hits(last, h))
        total = total + sums[0:128]
        rest = rest + sums[128:160]
        cover = cover + sums[163 + h : 164 + h] + sums[166 + h : 167 + h]
    cover = jnp.maximum(cover, 1.0)
    total = (total / cover).astype(BF)
    rest = (rest / cover).astype(BF)
    for q in range(MEM):
        out_ref[q, 0:128, :] = total
        out_ref[q, 128:160, :] = rest

    wide = last_t[112:128]
    lane = iota((ROWS, MESH * ROWS), 1)
    rows = jnp.concatenate(
        [jnp.where(lane % 16 == r, wide, jnp.zeros_like(wide)) for r in range(ROWS)], axis=0
    )
    tile = one_hot(
        iota((MESH * ROWS, PATCHES), 0) // 16 == iota((MESH * ROWS, PATCHES), 1) // 8
    )
    weight_ref[...] = dot(rows, tile)


def mixing_kernel(grid_ref, own_ref, weight_ref, got_ref, out_ref, inc_ref):
    for half in range(2):
        for lanes in range(PATCHES // 128):
            at = slice(128 * lanes, 128 * lanes + 128)
            mixed = [jnp.zeros((16, 128), F32) for _ in range(MEMBERS)]
            for m in range(MEM * MEMBERS):
                row = (half * MEMBERS + m % MEMBERS) * 16
                field = grid_ref[m // MEMBERS, row : row + 16, at].astype(F32)
                for n in range(MEMBERS):
                    w = (m % 16) * 16 + n * 3 + m // 16
                    mixed[n] = mixed[n] + weight_ref[w : w + 1, at] * field
            for n in range(MEMBERS):
                row = (half * MEMBERS + n) * 16
                inc_ref[row : row + 16, at] = mixed[n] - own_ref[0, row : row + 16, at].astype(F32)
    side = got_ref[:, :, 384:512].reshape(MESH * ROWS, 128).astype(F32)
    first = inc_ref[0:128, :].T.astype(BF)
    small = inc_ref[128:160, :]
    last = jnp.zeros((MESH * ROWS, 128), F32)
    for h in range(THIRDS):
        pad = [jnp.zeros((32, PATCHES), F32)] * 4
        pad[h] = small
        right = jnp.concatenate([first, jnp.concatenate(pad, axis=0).T.astype(BF)], axis=1)
        back = dot(hits(side, h), right)
        out_ref[:, :, 128 * h : 128 * h + 128] = back[:, 0:128].astype(BF).reshape(MESH, ROWS, 128)
        last = last + back[:, 128:256]
    out_ref[:, :, 384:512] = last.astype(BF).reshape(MESH, ROWS, 128)


def final_kernel(back_ref, ens_ref, spread_ref, out_ref):
    spread = spread_ref[...]
    area = dot_nt(jnp.ones((16, ELEMENTS), BF), spread)[0:1]
    scale = 1.0 / area
    for group in range(8):
        def turned(k):
            block = back_ref[8 * group : 8 * group + 8, :, 128 * k : 128 * k + 128]
            return block.reshape(128, 128).astype(F32).T

        first = jnp.concatenate([turned(h) for h in range(THIRDS)], axis=1)
        last = turned(3)
        last = jnp.concatenate([last[32 * h : 32 * h + 32] for h in range(THIRDS)], axis=1)
        left = jnp.concatenate([first, last], axis=0).astype(BF)
        correction = dot_nt(left, spread) * scale
        for k, (half, m, start) in enumerate(member_tiles(group)):
            if start < CHANNELS:
                value = ens_ref[m, start : start + 16, :].astype(F32) + correction[16 * k : 16 * k + 16]
                out_ref[m, start : start + 16, :] = value.astype(BF)


def vmem():
    return pl.BlockSpec(memory_space=pltpu.VMEM)


def call(kernel, outs, ins, scratch=(), limit=VMEM_BYTES):
    return pl.pallas_call(
        kernel,
        out_shape=[jax.ShapeDtypeStruct(s, d) for s, d in outs],
        in_specs=ins,
        out_specs=[vmem() for _ in outs],
        scratch_shapes=list(scratch),
        compiler_params=pltpu.CompilerParams(vmem_limit_bytes=limit),
    )


def shards(ensemble, ovl_owner, ovl_patch, ovl_weight, letkf_weight):
    margin = ovl_weight.transpose(1, 2, 3, 0).reshape(256, 24)
    mem = lax.axis_index("mem").astype(jnp.int32).reshape(1)
    send, spread = call(
        source_kernel,
        [((MESH, ROWS, WIDTH), BF), ((ELEMENTS, ELEMENTS), BF)],
        [pl.BlockSpec(memory_space=pltpu.SMEM)] + [pl.BlockSpec(memory_space=pltpu.HBM)] * 5,
        [
            pltpu.VMEM((MEMBERS, CHANNELS, ELEMENTS), BF),
            pltpu.VMEM((256, 24), BF),
            pltpu.VMEM((2, 24), jnp.int32),
            pltpu.VMEM((2, 24), jnp.int32),
            pltpu.VMEM((MEM * MEMBERS, MEM * MEMBERS), F32),
            pltpu.SemaphoreType.DMA((5,)),
        ],
        SOURCE_VMEM_BYTES,
    )(mem, ensemble, margin, ovl_owner.T, ovl_patch.T, letkf_weight[0])
    got = lax.all_to_all(send, "mesh", split_axis=0, concat_axis=0, tiled=True)
    copies, weight = call(
        patch_kernel, [((MEM, COLUMNS, PATCHES), BF), ((256, PATCHES), F32)], [vmem()]
    )(got)
    grid = lax.all_to_all(copies, "mem", split_axis=0, concat_axis=0, tiled=True)
    (back,) = call(
        mixing_kernel,
        [((MESH, ROWS, WIDTH), BF)],
        [vmem()] * 4,
        [pltpu.VMEM((COLUMNS, PATCHES), F32)],
    )(grid, copies, weight, got)
    returned = lax.all_to_all(back, "mesh", split_axis=0, concat_axis=0, tiled=True)
    (analysis,) = call(final_kernel, [((MEMBERS, CHANNELS, ELEMENTS), BF)], [vmem()] * 3)(
        returned, ensemble, spread
    )
    return analysis


def solution(mesh):
    in_specs = (
        P("mem", None, "mesh"),
        P("mesh", None),
        P("mesh", None),
        P("mesh", None, None, None),
        P("mesh", None, None),
    )
    out_specs = P("mem", None, "mesh")
    return jax.shard_map(shards, mesh=mesh, in_specs=in_specs, out_specs=out_specs, check_vma=False)
```

```python
import jax
import jax.numpy as jnp
from jax import lax
from jax.experimental import pallas as pl
from jax.experimental.pallas import tpu as pltpu
from jax.sharding import PartitionSpec as P

MESH = 64
MEM = 8
MEMBERS = 5
CHANNELS = 240
ELEMENTS = 384
CELLS = 8
PATCHES = 512
ROWS = 16
THIRDS = 3
WIDTH = 512
SIDE = 96
BF = jnp.bfloat16
F32 = jnp.float32
VMEM_BYTES = 40 * 1024 * 1024
SOURCE_VMEM_BYTES = 60 * 1024 * 1024


def iota(shape, dim):
    return lax.broadcasted_iota(jnp.int32, shape, dim)


def dot(a, b):
    return jnp.dot(a, b, preferred_element_type=F32)


def dot_nt(a, b):
    return lax.dot_general(a, b, (((1,), (1,)), ((), ())), preferred_element_type=F32)


def one_hot(mask):
    return jnp.where(mask, 1.0, 0.0).astype(BF)


def member_tiles(group):
    return [(half, m, group * 32 + half * 16) for half in range(2) for m in range(MEMBERS)]


def source_kernel(mem_ref, *refs):
    sources, (out_ref, spread_ref), landed, sems = refs[:5], refs[5:7], refs[7:12], refs[12]
    copies = [pltpu.make_async_copy(a, b, sems.at[k]) for k, (a, b) in enumerate(zip(sources, landed))]
    for copy in copies:
        copy.start()
    for copy in copies[1:]:
        copy.wait()
    ens_ref, margin_ref, owner_ref, patch_ref, letkf_ref = landed
    lane24 = iota((24, ELEMENTS), 1)
    block_of = (lane24 // 128) * 8 + lane24 % 8
    pick_block = iota((24, ELEMENTS), 0) == block_of
    expanded = dot(margin_ref[...], one_hot(pick_block))
    row = iota((256, ELEMENTS), 0)
    lane = iota((256, ELEMENTS), 1)
    fits = (row // 128 == (lane % 16) // 8) & (row % 8 == (lane % 128) // 16)
    expanded = jnp.where(fits, expanded, 0.0).astype(BF)
    fold = one_hot((iota((ELEMENTS, 256), 1) % 128) // 8 == iota((ELEMENTS, 256), 0) % 16)
    spread = dot(fold, expanded)
    er = iota((ELEMENTS, ELEMENTS), 0)
    el = iota((ELEMENTS, ELEMENTS), 1)
    spread = jnp.where(er // 16 == (el // 128) * 8 + el % 8, spread, 0.0)
    sums = jnp.sum(spread, axis=0, keepdims=True)
    spread = spread.astype(BF)
    spread_ref[...] = spread
    high = sums.astype(BF).astype(F32)
    low = sums - high

    dest = owner_ref[...] * 8 + patch_ref[...] - 256
    dest = dest.astype(F32).astype(BF)
    place = dot(dest, one_hot(pick_block))
    lane2 = iota((2, ELEMENTS), 1)
    place = jnp.sum(jnp.where((lane2 % 16) // 8 == iota((2, ELEMENTS), 0), place, 0.0), axis=0, keepdims=True)

    own = mem_ref[0] * MEMBERS
    pick_own = one_hot((iota((16, 40), 1) == own + iota((16, 40), 0) // 3) & (iota((16, 40), 0) < 15))
    mine = dot_nt(pick_own, letkf_ref[...].astype(BF))
    keep = (iota((16, 40), 1) // 16) == iota((16, 40), 0) % 3
    mine = jnp.where(keep, mine, 0.0).astype(BF)
    weights = dot(mine, one_hot(iota((40, 128), 0) % 16 == iota((40, 128), 1) % 16))

    def parts(value):
        return [value[:, 128 * h : 128 * h + 128] for h in range(THIRDS)]

    side = jnp.concatenate(
        parts(place) + parts(high) + parts(low) + [jnp.zeros((7, 128), F32), weights], axis=0
    )

    copies[0].wait()
    for group in range(8):
        tiles = []
        for half, m, start in member_tiles(group):
            if start < CHANNELS:
                tiles.append(ens_ref[m, start : start + 16, :])
            else:
                tiles.append(jnp.zeros((16, ELEMENTS), BF))
        pieces = dot(jnp.concatenate(tiles, axis=0), spread)
        for h in range(THIRDS):
            block = pieces[0:128, 128 * h : 128 * h + 128].T.astype(BF)
            out_ref[8 * group : 8 * group + 8, :, 128 * h : 128 * h + 128] = block.reshape(8, ROWS, 128)
        rest = jnp.concatenate(parts(pieces[128:160]) + [side], axis=0)
        out_ref[8 * group : 8 * group + 8, :, 384:512] = rest.T.astype(BF).reshape(8, ROWS, 128)


def hits(side, h):
    place = side[:, SIDE + h : SIDE + h + 1].astype(F32) + 256.0
    lanes = iota((MESH * ROWS, PATCHES), 1).astype(F32)
    return one_hot(lanes == place)


def patch_kernel(got_ref, out_ref):
    got = got_ref[...].reshape(MESH * ROWS, WIDTH)
    last = got[:, 384:512].astype(F32)
    last_t = last.T.astype(BF)
    total = jnp.zeros((128, PATCHES), F32)
    rest = jnp.zeros((32, PATCHES), F32)
    cover = jnp.zeros((1, PATCHES), F32)
    for h in range(THIRDS):
        first_t = got[:, 128 * h : 128 * h + 128].astype(F32).T.astype(BF)
        left = jnp.concatenate([first_t, last_t[32 * h : 32 * h + 32], last_t[96:112]], axis=0)
        sums = dot(left, hits(last, h))
        total = total + sums[0:128]
        rest = rest + sums[128:160]
        cover = cover + sums[163 + h : 164 + h] + sums[166 + h : 167 + h]
    cover = jnp.maximum(cover, 1.0)
    grid = jnp.concatenate([total, rest], axis=0) / cover
    for q in range(MEM):
        at = slice(64 * q, 64 * q + 64)
        out_ref[q, 0:80, :] = jnp.concatenate([grid[0:80, at], grid[80:160, at]], axis=1).astype(BF)
        out_ref[q, 80:96, :] = last_t[112:128, 128 * q : 128 * q + 128]


def mixing_kernel(got_ref, out_ref, weight_ref, field_ref):
    tile = one_hot(iota((128, 128), 0) // 16 == (iota((128, 128), 1) % 64) // 8)
    lane = iota((ROWS, 128), 1)
    for q in range(MEM):
        wide = got_ref[q, 80:96, :]
        rows = [jnp.where(lane % 16 == r, wide, jnp.zeros_like(wide)) for r in range(ROWS)]
        weight_ref[q] = dot(jnp.concatenate(rows, axis=0), tile)
        field_ref[q] = got_ref[q, 0:80, :].astype(F32)

    def mix(q, carry):
        mixed = [jnp.zeros((16, 128), F32) for _ in range(MEMBERS)]
        for m in range(MEM * MEMBERS):
            row = (m % MEMBERS) * 16
            field = field_ref[m // MEMBERS, row : row + 16, :]
            for n in range(MEMBERS):
                w = (m % 16) * 16 + n * 3 + m // 16
                mixed[n] = mixed[n] + weight_ref[q, w : w + 1, :] * field
        for n in range(MEMBERS):
            out_ref[q, 16 * n : 16 * n + 16, :] = (mixed[n] - field_ref[q, 16 * n : 16 * n + 16, :]).astype(BF)
        return carry

    lax.fori_loop(0, MEM, mix, 0)


def expand_kernel(inc_ref, got_ref, out_ref):
    halves = [[], []]
    for q in range(0, MEM, 2):
        even, odd = inc_ref[q].astype(F32), inc_ref[q + 1].astype(F32)
        halves[0].append(jnp.concatenate([even[:, 0:64], odd[:, 0:64]], axis=1))
        halves[1].append(jnp.concatenate([even[:, 64:128], odd[:, 64:128]], axis=1))
    inc = jnp.concatenate([jnp.concatenate(half, axis=1) for half in halves], axis=0)
    side = got_ref[:, :, 384:512].reshape(MESH * ROWS, 128).astype(F32)
    first = inc[0:128].T.astype(BF)
    small = inc[128:160]
    last = jnp.zeros((MESH * ROWS, 128), F32)
    for h in range(THIRDS):
        pad = [jnp.zeros((32, PATCHES), F32)] * 4
        pad[h] = small
        right = jnp.concatenate([first, jnp.concatenate(pad, axis=0).T.astype(BF)], axis=1)
        back = dot(hits(side, h), right)
        out_ref[:, :, 128 * h : 128 * h + 128] = back[:, 0:128].astype(BF).reshape(MESH, ROWS, 128)
        last = last + back[:, 128:256]
    out_ref[:, :, 384:512] = last.astype(BF).reshape(MESH, ROWS, 128)


def final_kernel(back_ref, ens_ref, spread_ref, out_ref):
    spread = spread_ref[...]
    area = dot_nt(jnp.ones((16, ELEMENTS), BF), spread)[0:1]
    scale = 1.0 / area
    for group in range(8):
        def turned(k):
            block = back_ref[8 * group : 8 * group + 8, :, 128 * k : 128 * k + 128]
            return block.reshape(128, 128).astype(F32).T

        first = jnp.concatenate([turned(h) for h in range(THIRDS)], axis=1)
        last = turned(3)
        last = jnp.concatenate([last[32 * h : 32 * h + 32] for h in range(THIRDS)], axis=1)
        left = jnp.concatenate([first, last], axis=0).astype(BF)
        correction = dot_nt(left, spread) * scale
        for k, (half, m, start) in enumerate(member_tiles(group)):
            if start < CHANNELS:
                value = ens_ref[m, start : start + 16, :].astype(F32) + correction[16 * k : 16 * k + 16]
                out_ref[m, start : start + 16, :] = value.astype(BF)


def vmem():
    return pl.BlockSpec(memory_space=pltpu.VMEM)


def call(kernel, outs, ins, scratch=(), limit=VMEM_BYTES):
    return pl.pallas_call(
        kernel,
        out_shape=[jax.ShapeDtypeStruct(s, d) for s, d in outs],
        in_specs=ins,
        out_specs=[vmem() for _ in outs],
        scratch_shapes=list(scratch),
        compiler_params=pltpu.CompilerParams(vmem_limit_bytes=limit),
    )


def shards(ensemble, ovl_owner, ovl_patch, ovl_weight, letkf_weight):
    margin = ovl_weight.transpose(1, 2, 3, 0).reshape(256, 24)
    mem = lax.axis_index("mem").astype(jnp.int32).reshape(1)
    send, spread = call(
        source_kernel,
        [((MESH, ROWS, WIDTH), BF), ((ELEMENTS, ELEMENTS), BF)],
        [pl.BlockSpec(memory_space=pltpu.SMEM)] + [pl.BlockSpec(memory_space=pltpu.HBM)] * 5,
        [
            pltpu.VMEM((MEMBERS, CHANNELS, ELEMENTS), BF),
            pltpu.VMEM((256, 24), BF),
            pltpu.VMEM((2, 24), jnp.int32),
            pltpu.VMEM((2, 24), jnp.int32),
            pltpu.VMEM((MEM * MEMBERS, MEM * MEMBERS), F32),
            pltpu.SemaphoreType.DMA((5,)),
        ],
        SOURCE_VMEM_BYTES,
    )(mem, ensemble, margin, ovl_owner.T, ovl_patch.T, letkf_weight[0])
    got = lax.all_to_all(send, "mesh", split_axis=0, concat_axis=0, tiled=True)
    (fields,) = call(patch_kernel, [((MEM, 96, 128), BF)], [vmem()])(got)
    fields = lax.all_to_all(fields, "mem", split_axis=0, concat_axis=0, tiled=True)
    (mixed,) = call(
        mixing_kernel,
        [((MEM, 80, 128), BF)],
        [vmem()],
        [pltpu.VMEM((MEM, 256, 128), F32), pltpu.VMEM((MEM, 80, 128), F32)],
    )(fields)
    mixed = lax.all_to_all(mixed, "mem", split_axis=0, concat_axis=0, tiled=True)
    (back,) = call(expand_kernel, [((MESH, ROWS, WIDTH), BF)], [vmem()] * 2)(mixed, got)
    returned = lax.all_to_all(back, "mesh", split_axis=0, concat_axis=0, tiled=True)
    (analysis,) = call(final_kernel, [((MEMBERS, CHANNELS, ELEMENTS), BF)], [vmem()] * 3)(
        returned, ensemble, spread
    )
    return analysis


def solution(mesh):
    in_specs = (
        P("mem", None, "mesh"),
        P("mesh", None),
        P("mesh", None),
        P("mesh", None, None, None),
        P("mesh", None, None),
    )
    out_specs = P("mem", None, "mesh")
    return jax.shard_map(shards, mesh=mesh, in_specs=in_specs, out_specs=out_specs, check_vma=False)
```

```python
import jax
import jax.numpy as jnp
from jax import lax
from jax.experimental import pallas as pl
from jax.experimental.pallas import tpu as pltpu
from jax.sharding import PartitionSpec as P

MESH = 64
MEM = 8
MEMBERS = 5
CHANNELS = 240
ELEMENTS = 384
CELLS = 8
PATCHES = 512
ROWS = 16
THIRDS = 3
QUARTERS = 4
WIDTH = 1920
WIDE_ROWS = 1216
BF = jnp.bfloat16
F32 = jnp.float32
VMEM_BYTES = 40 * 1024 * 1024
SOURCE_VMEM_BYTES = 60 * 1024 * 1024


def iota(shape, dim):
    return lax.broadcasted_iota(jnp.int32, shape, dim)


def dot(a, b):
    return jnp.dot(a, b, preferred_element_type=F32)


def dot_nt(a, b):
    return lax.dot_general(a, b, (((1,), (1,)), ((), ())), preferred_element_type=F32)


def one_hot(mask):
    return jnp.where(mask, 1.0, 0.0).astype(BF)


def turn(value, shift):
    return pltpu.roll(value, shift, 2)


def pack(out_ref, at, firsts, last):
    for h in range(THIRDS):
        block = firsts[h]
        for a in range(QUARTERS):
            lanes = slice(128 * (3 * a + h), 128 * (3 * a + h) + 128)
            out_ref[at, :, lanes] = block[:, 4 * a : 4 * a + 4, :].astype(BF)
    n = last.shape[0]
    front = iota((n, 4, 128), 2) < 96
    for i in range(THIRDS):
        tail = turn(last, 96 - 32 * i)[:, 12:16, :]
        lanes = slice(128 * (12 + i), 128 * (12 + i) + 128)
        out_ref[at, :, lanes] = jnp.where(front, last[:, 4 * i : 4 * i + 4, :], tail).astype(BF)


def unpack(ref, at, h):
    parts = []
    for a in range(QUARTERS):
        lanes = slice(128 * (3 * a + h), 128 * (3 * a + h) + 128)
        parts.append(ref[at, :, lanes].astype(F32))
    return jnp.concatenate(parts, axis=1)


def unpack_last(ref, at):
    tiles = [ref[at, :, 128 * (12 + i) : 128 * (12 + i) + 128].astype(F32) for i in range(THIRDS)]
    lane = iota(tiles[0].shape, 2) // 32
    tail = turn(tiles[0], 32)
    for h in range(1, THIRDS):
        tail = jnp.where(lane == h, turn(tiles[h], 32 * h + 32), tail)
    return jnp.concatenate(tiles + [tail], axis=1)


def places(group):
    return [m * CHANNELS + 2 * group + parity for parity in range(2) for m in range(MEMBERS)]


def widen(ens_ref, wide_ref):
    for m in range(MEMBERS):
        for j in range(3):
            rows = slice(m * CHANNELS, (m + 1) * CHANNELS)
            wide_ref[j, rows, :] = ens_ref[m, :, 128 * j : 128 * j + 128].astype(F32)


def source_kernel(mem_ref, *refs):
    sources, (out_ref, spread_ref), landed, sems = refs[:5], refs[5:7], refs[7:12], refs[12]
    wide_ref = refs[13]
    copies = [pltpu.make_async_copy(a, b, sems.at[k]) for k, (a, b) in enumerate(zip(sources, landed))]
    for copy in copies:
        copy.start()
    for copy in copies[1:]:
        copy.wait()
    ens_ref, margin_ref, owner_ref, patch_ref, letkf_ref = landed
    lane24 = iota((24, ELEMENTS), 1)
    block_of = (lane24 // 128) * 8 + lane24 % 8
    pick_block = iota((24, ELEMENTS), 0) == block_of
    expanded = dot(margin_ref[...], one_hot(pick_block))
    row = iota((256, ELEMENTS), 0)
    lane = iota((256, ELEMENTS), 1)
    fits = (row // 128 == (lane % 16) // 8) & (row % 8 == (lane % 128) // 16)
    expanded = jnp.where(fits, expanded, 0.0).astype(BF)
    fold = one_hot((iota((ELEMENTS, 256), 1) % 128) // 8 == iota((ELEMENTS, 256), 0) % 16)
    spread = dot(fold, expanded)
    er = iota((ELEMENTS, ELEMENTS), 0)
    el = iota((ELEMENTS, ELEMENTS), 1)
    spread = jnp.where(er // 16 == (el // 128) * 8 + el % 8, spread, 0.0)
    sums = jnp.sum(spread, axis=0, keepdims=True)
    spread = spread.astype(BF)
    spread_ref[...] = spread
    high = sums.astype(BF).astype(F32)
    low = sums - high

    dest = owner_ref[...] * 8 + patch_ref[...] - 256
    dest = dest.astype(F32).astype(BF)
    place = dot(dest, one_hot(pick_block))
    lane2 = iota((2, ELEMENTS), 1)
    place = jnp.sum(jnp.where((lane2 % 16) // 8 == iota((2, ELEMENTS), 0), place, 0.0), axis=0, keepdims=True)

    own = mem_ref[0] * MEMBERS
    pick_own = one_hot((iota((16, 40), 1) == own + iota((16, 40), 0)) & (iota((16, 40), 0) < MEMBERS))
    mine = dot_nt(pick_own, letkf_ref[...].astype(BF)).astype(BF)
    lane40 = iota((40, ELEMENTS), 1)
    weights = dot(mine, one_hot(iota((40, ELEMENTS), 0) == (lane40 // 128) * 16 + lane40 % 16))
    sides = [place, high, low] + [weights[n : n + 1] for n in range(MEMBERS)] + [jnp.zeros_like(low)] * 2
    spare = iota((16, ELEMENTS), 0) == 15

    copies[0].wait()
    widen(ens_ref, wide_ref)
    for group in range(8):
        tiles = [
            jnp.concatenate([wide_ref[j, pl.ds(start, 16, 16), :] for j in range(3)], axis=1)
            for start in places(group)
        ]
        pieces = dot(jnp.concatenate(tiles, axis=0).astype(BF), spread)
        pieces = jnp.concatenate(
            [jnp.where(spare, sides[k], pieces[16 * k : 16 * k + 16]) for k in range(10)], axis=0
        )
        firsts = [pieces[0:128, 128 * h : 128 * h + 128].T.reshape(8, ROWS, 128) for h in range(THIRDS)]
        rest = [pieces[128:160, 128 * h : 128 * h + 128] for h in range(THIRDS)]
        rest = jnp.concatenate(rest + [jnp.zeros((32, 128), F32)], axis=0)
        pack(out_ref, slice(8 * group, 8 * group + 8), firsts, rest.T.reshape(8, ROWS, 128))


def hits(first):
    place = first[:, 15:16] + 256.0
    lanes = iota((MESH * ROWS, PATCHES), 1).astype(F32)
    return one_hot(lanes == place)


def patch_kernel(got_ref, out_ref):
    every = slice(0, MESH)
    last_t = unpack_last(got_ref, every).reshape(MESH * ROWS, 128).T
    grid = jnp.zeros((160, PATCHES), F32)
    weights = [[None] * THIRDS for _ in range(MEMBERS)]
    for h in range(THIRDS):
        first = unpack(got_ref, every, h).reshape(MESH * ROWS, 128)
        first_t = first.T
        left = jnp.concatenate([first_t, last_t[32 * h : 32 * h + 32]], axis=0).astype(BF)
        grid = grid + dot(left, hits(first))
        for n in range(MEMBERS):
            weights[n][h] = first_t[63 + 16 * n : 64 + 16 * n]
    cover = grid[31:32] + grid[47:48]
    weights = sum(weights, []) + [jnp.zeros((1, MESH * ROWS), F32)]
    weights = jnp.concatenate(weights, axis=0).astype(BF)
    cover = jnp.maximum(cover, 1.0)
    grid = grid / cover
    for q in range(MEM):
        at = slice(64 * q, 64 * q + 64)
        out_ref[q, 0:80, :] = jnp.concatenate([grid[0:80, at], grid[80:160, at]], axis=1).astype(BF)
        out_ref[q, 80:96, :] = weights[:, 128 * q : 128 * q + 128]


def mixing_kernel(got_ref, out_ref, weight_ref, field_ref):
    tile = one_hot(iota((128, 128), 0) // 16 == (iota((128, 128), 1) % 64) // 8)
    lane = iota((ROWS, 128), 1)
    for q in range(MEM):
        wide = got_ref[q, 80:96, :]
        rows = [jnp.where(lane % 16 == r, wide, jnp.zeros_like(wide)) for r in range(ROWS)]
        weight_ref[q] = dot(jnp.concatenate(rows, axis=0), tile)
        field_ref[q] = got_ref[q, 0:80, :].astype(F32)

    def mix(q, carry):
        mixed = [jnp.zeros((16, 128), F32) for _ in range(MEMBERS)]
        for m in range(MEM * MEMBERS):
            row = (m % MEMBERS) * 16
            field = field_ref[m // MEMBERS, row : row + 16, :]
            for n in range(MEMBERS):
                w = (m % 16) * 16 + n * 3 + m // 16
                mixed[n] = mixed[n] + weight_ref[q, w : w + 1, :] * field
        for n in range(MEMBERS):
            out_ref[q, 16 * n : 16 * n + 16, :] = (mixed[n] - field_ref[q, 16 * n : 16 * n + 16, :]).astype(BF)
        return carry

    lax.fori_loop(0, MEM, mix, 0)


def expand_kernel(inc_ref, got_ref, out_ref):
    halves = [[], []]
    for q in range(0, MEM, 2):
        even, odd = inc_ref[q].astype(F32), inc_ref[q + 1].astype(F32)
        halves[0].append(jnp.concatenate([even[:, 0:64], odd[:, 0:64]], axis=1))
        halves[1].append(jnp.concatenate([even[:, 64:128], odd[:, 64:128]], axis=1))
    inc = jnp.concatenate([jnp.concatenate(half, axis=1) for half in halves], axis=0)
    first = inc[0:128].T.astype(BF)
    small = inc[128:160]
    last = jnp.zeros((MESH * ROWS, 128), F32)
    every = slice(0, MESH)
    firsts = []
    for h in range(THIRDS):
        pad = [jnp.zeros((32, PATCHES), F32)] * 4
        pad[h] = small
        right = jnp.concatenate([first, jnp.concatenate(pad, axis=0).T.astype(BF)], axis=1)
        back = dot(hits(unpack(got_ref, every, h).reshape(MESH * ROWS, 128)), right)
        firsts.append(back[:, 0:128].reshape(MESH, ROWS, 128))
        last = last + back[:, 128:256]
    pack(out_ref, every, firsts, last.reshape(MESH, ROWS, 128))


def final_kernel(back_ref, ens_ref, spread_ref, out_ref, wide_ref):
    spread = spread_ref[...]
    area = dot_nt(jnp.ones((16, ELEMENTS), BF), spread)[0:1]
    scale = 1.0 / area
    widen(ens_ref, wide_ref)
    for group in range(8):
        at = slice(8 * group, 8 * group + 8)
        first = jnp.concatenate([unpack(back_ref, at, h).reshape(128, 128).T for h in range(THIRDS)], axis=1)
        last = unpack_last(back_ref, at).reshape(128, 128).T
        last = jnp.concatenate([last[32 * h : 32 * h + 32] for h in range(THIRDS)], axis=1)
        left = jnp.concatenate([first, last], axis=0).astype(BF)
        correction = dot_nt(left, spread) * scale
        for k, start in enumerate(places(group)):
            rows = pl.ds(start, 15, 16)
            for j in range(3):
                change = correction[16 * k : 16 * k + 15, 128 * j : 128 * j + 128]
                wide_ref[j, rows, :] = wide_ref[j, rows, :] + change
    for m in range(MEMBERS):
        for j in range(3):
            rows = slice(m * CHANNELS, (m + 1) * CHANNELS)
            out_ref[m, :, 128 * j : 128 * j + 128] = wide_ref[j, rows, :].astype(BF)


def vmem():
    return pl.BlockSpec(memory_space=pltpu.VMEM)


def call(kernel, outs, ins, scratch=(), limit=VMEM_BYTES):
    return pl.pallas_call(
        kernel,
        out_shape=[jax.ShapeDtypeStruct(s, d) for s, d in outs],
        in_specs=ins,
        out_specs=[vmem() for _ in outs],
        scratch_shapes=list(scratch),
        compiler_params=pltpu.CompilerParams(vmem_limit_bytes=limit),
    )


def shards(ensemble, ovl_owner, ovl_patch, ovl_weight, letkf_weight):
    margin = ovl_weight.transpose(1, 2, 3, 0).reshape(256, 24)
    mem = lax.axis_index("mem").astype(jnp.int32).reshape(1)
    send, spread = call(
        source_kernel,
        [((MESH, QUARTERS, WIDTH), BF), ((ELEMENTS, ELEMENTS), BF)],
        [pl.BlockSpec(memory_space=pltpu.SMEM)] + [pl.BlockSpec(memory_space=pltpu.HBM)] * 5,
        [
            pltpu.VMEM((MEMBERS, CHANNELS, ELEMENTS), BF),
            pltpu.VMEM((256, 24), BF),
            pltpu.VMEM((2, 24), jnp.int32),
            pltpu.VMEM((2, 24), jnp.int32),
            pltpu.VMEM((MEM * MEMBERS, MEM * MEMBERS), F32),
            pltpu.SemaphoreType.DMA((5,)),
            pltpu.VMEM((3, WIDE_ROWS, 128), F32),
        ],
        SOURCE_VMEM_BYTES,
    )(mem, ensemble, margin, ovl_owner.T, ovl_patch.T, letkf_weight[0])
    got = lax.all_to_all(send, "mesh", split_axis=0, concat_axis=0, tiled=True)
    (fields,) = call(patch_kernel, [((MEM, 96, 128), BF)], [vmem()])(got)
    fields = lax.all_to_all(fields, "mem", split_axis=0, concat_axis=0, tiled=True)
    (mixed,) = call(
        mixing_kernel,
        [((MEM, 80, 128), BF)],
        [vmem()],
        [pltpu.VMEM((MEM, 256, 128), F32), pltpu.VMEM((MEM, 80, 128), F32)],
    )(fields)
    mixed = lax.all_to_all(mixed, "mem", split_axis=0, concat_axis=0, tiled=True)
    (back,) = call(expand_kernel, [((MESH, QUARTERS, WIDTH), BF)], [vmem()] * 2)(mixed, got)
    returned = lax.all_to_all(back, "mesh", split_axis=0, concat_axis=0, tiled=True)
    (analysis,) = call(
        final_kernel,
        [((MEMBERS, CHANNELS, ELEMENTS), BF)],
        [vmem()] * 3,
        [pltpu.VMEM((3, WIDE_ROWS, 128), F32)],
    )(returned, ensemble, spread)
    return analysis


def solution(mesh):
    in_specs = (
        P("mem", None, "mesh"),
        P("mesh", None),
        P("mesh", None),
        P("mesh", None, None, None),
        P("mesh", None, None),
    )
    out_specs = P("mem", None, "mesh")
    return jax.shard_map(shards, mesh=mesh, in_specs=in_specs, out_specs=out_specs, check_vma=False)
```

```python
import jax
import jax.numpy as jnp
from jax import lax
from jax.experimental import pallas as pl
from jax.experimental.pallas import tpu as pltpu
from jax.sharding import PartitionSpec as P

MESH = 64
MEM = 8
MEMBERS = 5
CHANNELS = 240
ELEMENTS = 384
CELLS = 8
PATCHES = 512
ROWS = 16
THIRDS = 3
QUARTERS = 4
WIDTH = 1920
WIDE_ROWS = 1216
BF = jnp.bfloat16
F32 = jnp.float32
VMEM_BYTES = 40 * 1024 * 1024
SOURCE_VMEM_BYTES = 60 * 1024 * 1024


def iota(shape, dim):
    return lax.broadcasted_iota(jnp.int32, shape, dim)


def dot(a, b):
    return jnp.dot(a, b, preferred_element_type=F32)


def dot_nt(a, b):
    return lax.dot_general(a, b, (((1,), (1,)), ((), ())), preferred_element_type=F32)


def one_hot(mask):
    return jnp.where(mask, 1.0, 0.0).astype(BF)


def turn(value, shift):
    return pltpu.roll(value, shift, 2)


def pack(out_ref, at, firsts, last):
    for h in range(THIRDS):
        block = firsts[h]
        for a in range(QUARTERS):
            lanes = slice(128 * (3 * a + h), 128 * (3 * a + h) + 128)
            out_ref[at, :, lanes] = block[:, 4 * a : 4 * a + 4, :].astype(BF)
    n = last.shape[0]
    front = iota((n, 4, 128), 2) < 96
    for i in range(THIRDS):
        tail = turn(last, 96 - 32 * i)[:, 12:16, :]
        lanes = slice(128 * (12 + i), 128 * (12 + i) + 128)
        out_ref[at, :, lanes] = jnp.where(front, last[:, 4 * i : 4 * i + 4, :], tail).astype(BF)


def unpack(ref, at, h):
    parts = []
    for a in range(QUARTERS):
        lanes = slice(128 * (3 * a + h), 128 * (3 * a + h) + 128)
        parts.append(ref[at, :, lanes].astype(F32))
    return jnp.concatenate(parts, axis=1)


def unpack_last(ref, at):
    tiles = [ref[at, :, 128 * (12 + i) : 128 * (12 + i) + 128].astype(F32) for i in range(THIRDS)]
    lane = iota(tiles[0].shape, 2) // 32
    tail = turn(tiles[0], 32)
    for h in range(1, THIRDS):
        tail = jnp.where(lane == h, turn(tiles[h], 32 * h + 32), tail)
    return jnp.concatenate(tiles + [tail], axis=1)


def places(group):
    return [m * CHANNELS + 2 * group + parity for parity in range(2) for m in range(MEMBERS)]


def source_kernel(mem_ref, *refs):
    ens_hbm, small, (out_hbm, spread_hbm), landed = refs[0], refs[1:5], refs[5:7], refs[8:12]
    ens_ref, wide_ref, out_ref, spread_ref, in_sems, out_sems = refs[7], *refs[12:17]
    fetches = [pltpu.make_async_copy(a, b, in_sems.at[k]) for k, (a, b) in enumerate(zip(small, landed))]
    members = [
        pltpu.make_async_copy(ens_hbm.at[m], ens_ref.at[m], in_sems.at[4 + m]) for m in range(MEMBERS)
    ]
    for copy in fetches + members:
        copy.start()
    for copy in fetches:
        copy.wait()
    margin_ref, owner_ref, patch_ref, letkf_ref = landed
    lane24 = iota((24, ELEMENTS), 1)
    block_of = (lane24 // 128) * 8 + lane24 % 8
    pick_block = iota((24, ELEMENTS), 0) == block_of
    expanded = dot(margin_ref[...], one_hot(pick_block))
    row = iota((256, ELEMENTS), 0)
    lane = iota((256, ELEMENTS), 1)
    fits = (row // 128 == (lane % 16) // 8) & (row % 8 == (lane % 128) // 16)
    expanded = jnp.where(fits, expanded, 0.0).astype(BF)
    fold = one_hot((iota((ELEMENTS, 256), 1) % 128) // 8 == iota((ELEMENTS, 256), 0) % 16)
    spread = dot(fold, expanded)
    er = iota((ELEMENTS, ELEMENTS), 0)
    el = iota((ELEMENTS, ELEMENTS), 1)
    spread = jnp.where(er // 16 == (el // 128) * 8 + el % 8, spread, 0.0)
    sums = jnp.sum(spread, axis=0, keepdims=True)
    spread = spread.astype(BF)
    spread_ref[...] = spread
    leaving = [pltpu.make_async_copy(spread_ref, spread_hbm, out_sems.at[8])]
    leaving[0].start()
    high = sums.astype(BF).astype(F32)
    low = sums - high

    dest = owner_ref[...] * 8 + patch_ref[...] - 256
    dest = dest.astype(F32).astype(BF)
    place = dot(dest, one_hot(pick_block))
    lane2 = iota((2, ELEMENTS), 1)
    place = jnp.sum(jnp.where((lane2 % 16) // 8 == iota((2, ELEMENTS), 0), place, 0.0), axis=0, keepdims=True)

    own = mem_ref[0] * MEMBERS
    pick_own = one_hot((iota((16, 40), 1) == own + iota((16, 40), 0)) & (iota((16, 40), 0) < MEMBERS))
    mine = dot_nt(pick_own, letkf_ref[...].astype(BF)).astype(BF)
    lane40 = iota((40, ELEMENTS), 1)
    weights = dot(mine, one_hot(iota((40, ELEMENTS), 0) == (lane40 // 128) * 16 + lane40 % 16))
    sides = [place, high, low] + [weights[n : n + 1] for n in range(MEMBERS)] + [jnp.zeros_like(low)] * 2
    spare = iota((16, ELEMENTS), 0) == 15

    for m in range(MEMBERS):
        members[m].wait()
        for j in range(3):
            rows = slice(m * CHANNELS, (m + 1) * CHANNELS)
            wide_ref[j, rows, :] = ens_ref[m, :, 128 * j : 128 * j + 128].astype(F32)
    for group in range(8):
        tiles = [
            jnp.concatenate([wide_ref[j, pl.ds(start, 16, 16), :] for j in range(3)], axis=1)
            for start in places(group)
        ]
        pieces = dot(jnp.concatenate(tiles, axis=0).astype(BF), spread)
        pieces = jnp.concatenate(
            [jnp.where(spare, sides[k], pieces[16 * k : 16 * k + 16]) for k in range(10)], axis=0
        )
        firsts = [pieces[0:128, 128 * h : 128 * h + 128].T.reshape(8, ROWS, 128) for h in range(THIRDS)]
        rest = [pieces[128:160, 128 * h : 128 * h + 128] for h in range(THIRDS)]
        rest = jnp.concatenate(rest + [jnp.zeros((32, 128), F32)], axis=0)
        pack(out_ref, slice(8 * group, 8 * group + 8), firsts, rest.T.reshape(8, ROWS, 128))
        part = pl.ds(8 * group, 8)
        leaving.append(pltpu.make_async_copy(out_ref.at[part], out_hbm.at[part], out_sems.at[group]))
        leaving[-1].start()
    for copy in leaving:
        copy.wait()


def hits(first):
    place = first[:, 15:16] + 256.0
    lanes = iota((MESH * ROWS, PATCHES), 1).astype(F32)
    return one_hot(lanes == place)


def patch_kernel(got_ref, out_ref):
    every = slice(0, MESH)
    last_t = unpack_last(got_ref, every).reshape(MESH * ROWS, 128).T
    grid = jnp.zeros((160, PATCHES), F32)
    weights = [[None] * THIRDS for _ in range(MEMBERS)]
    for h in range(THIRDS):
        first = unpack(got_ref, every, h).reshape(MESH * ROWS, 128)
        first_t = first.T
        left = jnp.concatenate([first_t, last_t[32 * h : 32 * h + 32]], axis=0).astype(BF)
        grid = grid + dot(left, hits(first))
        for n in range(MEMBERS):
            weights[n][h] = first_t[63 + 16 * n : 64 + 16 * n]
    cover = grid[31:32] + grid[47:48]
    weights = sum(weights, []) + [jnp.zeros((1, MESH * ROWS), F32)]
    weights = jnp.concatenate(weights, axis=0).astype(BF)
    cover = jnp.maximum(cover, 1.0)
    grid = grid / cover
    for q in range(MEM):
        at = slice(64 * q, 64 * q + 64)
        out_ref[q, 0:80, :] = jnp.concatenate([grid[0:80, at], grid[80:160, at]], axis=1).astype(BF)
        out_ref[q, 80:96, :] = weights[:, 128 * q : 128 * q + 128]


def mixing_kernel(got_ref, out_ref, weight_ref, field_ref):
    tile = one_hot(iota((128, 128), 0) // 16 == (iota((128, 128), 1) % 64) // 8)
    lane = iota((ROWS, 128), 1)
    for q in range(MEM):
        wide = got_ref[q, 80:96, :]
        rows = [jnp.where(lane % 16 == r, wide, jnp.zeros_like(wide)) for r in range(ROWS)]
        weight_ref[q] = dot(jnp.concatenate(rows, axis=0), tile)
        field_ref[q] = got_ref[q, 0:80, :].astype(F32)

    def mix(q, carry):
        mixed = [jnp.zeros((16, 128), F32) for _ in range(MEMBERS)]
        for m in range(MEM * MEMBERS):
            row = (m % MEMBERS) * 16
            field = field_ref[m // MEMBERS, row : row + 16, :]
            for n in range(MEMBERS):
                w = (m % 16) * 16 + n * 3 + m // 16
                mixed[n] = mixed[n] + weight_ref[q, w : w + 1, :] * field
        for n in range(MEMBERS):
            out_ref[q, 16 * n : 16 * n + 16, :] = (mixed[n] - field_ref[q, 16 * n : 16 * n + 16, :]).astype(BF)
        return carry

    lax.fori_loop(0, MEM, mix, 0)


def expand_kernel(inc_ref, got_ref, out_ref):
    halves = [[], []]
    for q in range(0, MEM, 2):
        even, odd = inc_ref[q].astype(F32), inc_ref[q + 1].astype(F32)
        halves[0].append(jnp.concatenate([even[:, 0:64], odd[:, 0:64]], axis=1))
        halves[1].append(jnp.concatenate([even[:, 64:128], odd[:, 64:128]], axis=1))
    inc = jnp.concatenate([jnp.concatenate(half, axis=1) for half in halves], axis=0)
    first = inc[0:128].T.astype(BF)
    small = inc[128:160]
    last = jnp.zeros((MESH * ROWS, 128), F32)
    every = slice(0, MESH)
    firsts = []
    for h in range(THIRDS):
        pad = [jnp.zeros((32, PATCHES), F32)] * 4
        pad[h] = small
        right = jnp.concatenate([first, jnp.concatenate(pad, axis=0).T.astype(BF)], axis=1)
        back = dot(hits(unpack(got_ref, every, h).reshape(MESH * ROWS, 128)), right)
        firsts.append(back[:, 0:128].reshape(MESH, ROWS, 128))
        last = last + back[:, 128:256]
    pack(out_ref, every, firsts, last.reshape(MESH, ROWS, 128))


def final_kernel(back_ref, ens_ref, spread_ref, out_hbm, wide_ref, out_ref, sems):
    spread = spread_ref[...]
    area = dot_nt(jnp.ones((16, ELEMENTS), BF), spread)[0:1]
    scale = 1.0 / area
    for group in range(8):
        at = slice(8 * group, 8 * group + 8)
        first = jnp.concatenate([unpack(back_ref, at, h).reshape(128, 128).T for h in range(THIRDS)], axis=1)
        last = unpack_last(back_ref, at).reshape(128, 128).T
        last = jnp.concatenate([last[32 * h : 32 * h + 32] for h in range(THIRDS)], axis=1)
        left = jnp.concatenate([first, last], axis=0).astype(BF)
        correction = dot_nt(left, spread) * scale
        for k, start in enumerate(places(group)):
            for j in range(3):
                wide_ref[j, pl.ds(start, 15, 16), :] = correction[
                    16 * k : 16 * k + 15, 128 * j : 128 * j + 128
                ]
    copies = []
    for m in range(MEMBERS):
        for j in range(3):
            rows = slice(m * CHANNELS, (m + 1) * CHANNELS)
            lanes = slice(128 * j, 128 * j + 128)
            out_ref[m, :, lanes] = (ens_ref[m, :, lanes].astype(F32) + wide_ref[j, rows, :]).astype(BF)
        copies.append(pltpu.make_async_copy(out_ref.at[m], out_hbm.at[m], sems.at[m]))
        copies[-1].start()
    for copy in copies:
        copy.wait()


def vmem():
    return pl.BlockSpec(memory_space=pltpu.VMEM)


def hbm():
    return pl.BlockSpec(memory_space=pltpu.HBM)


def call(kernel, outs, ins, scratch=(), limit=VMEM_BYTES, place=vmem):
    return pl.pallas_call(
        kernel,
        out_shape=[jax.ShapeDtypeStruct(s, d) for s, d in outs],
        in_specs=ins,
        out_specs=[place() for _ in outs],
        scratch_shapes=list(scratch),
        compiler_params=pltpu.CompilerParams(vmem_limit_bytes=limit),
    )


def shards(ensemble, ovl_owner, ovl_patch, ovl_weight, letkf_weight):
    margin = ovl_weight.transpose(1, 2, 3, 0).reshape(256, 24)
    mem = lax.axis_index("mem").astype(jnp.int32).reshape(1)
    send, spread = call(
        source_kernel,
        [((MESH, QUARTERS, WIDTH), BF), ((ELEMENTS, ELEMENTS), BF)],
        [pl.BlockSpec(memory_space=pltpu.SMEM)] + [hbm()] * 5,
        [
            pltpu.VMEM((MEMBERS, CHANNELS, ELEMENTS), BF),
            pltpu.VMEM((256, 24), BF),
            pltpu.VMEM((2, 24), jnp.int32),
            pltpu.VMEM((2, 24), jnp.int32),
            pltpu.VMEM((MEM * MEMBERS, MEM * MEMBERS), F32),
            pltpu.VMEM((3, WIDE_ROWS, 128), F32),
            pltpu.VMEM((MESH, QUARTERS, WIDTH), BF),
            pltpu.VMEM((ELEMENTS, ELEMENTS), BF),
            pltpu.SemaphoreType.DMA((9,)),
            pltpu.SemaphoreType.DMA((9,)),
        ],
        SOURCE_VMEM_BYTES,
        hbm,
    )(mem, ensemble, margin, ovl_owner.T, ovl_patch.T, letkf_weight[0])
    got = lax.all_to_all(send, "mesh", split_axis=0, concat_axis=0, tiled=True)
    (fields,) = call(patch_kernel, [((MEM, 96, 128), BF)], [vmem()])(got)
    fields = lax.all_to_all(fields, "mem", split_axis=0, concat_axis=0, tiled=True)
    (mixed,) = call(
        mixing_kernel,
        [((MEM, 80, 128), BF)],
        [vmem()],
        [pltpu.VMEM((MEM, 256, 128), F32), pltpu.VMEM((MEM, 80, 128), F32)],
    )(fields)
    mixed = lax.all_to_all(mixed, "mem", split_axis=0, concat_axis=0, tiled=True)
    (back,) = call(expand_kernel, [((MESH, QUARTERS, WIDTH), BF)], [vmem()] * 2)(mixed, got)
    returned = lax.all_to_all(back, "mesh", split_axis=0, concat_axis=0, tiled=True)
    (analysis,) = call(
        final_kernel,
        [((MEMBERS, CHANNELS, ELEMENTS), BF)],
        [vmem()] * 3,
        [
            pltpu.VMEM((3, WIDE_ROWS, 128), F32),
            pltpu.VMEM((MEMBERS, CHANNELS, ELEMENTS), BF),
            pltpu.SemaphoreType.DMA((MEMBERS,)),
        ],
        place=hbm,
    )(returned, ensemble, spread)
    return analysis


def solution(mesh):
    in_specs = (
        P("mem", None, "mesh"),
        P("mesh", None),
        P("mesh", None),
        P("mesh", None, None, None),
        P("mesh", None, None),
    )
    out_specs = P("mem", None, "mesh")
    return jax.shard_map(shards, mesh=mesh, in_specs=in_specs, out_specs=out_specs, check_vma=False)
```

```python
import jax
import jax.numpy as jnp
from jax import lax
from jax.experimental import pallas as pl
from jax.experimental.pallas import tpu as pltpu
from jax.sharding import PartitionSpec as P

MESH = 64
MEM = 8
MEMBERS = 5
CHANNELS = 240
ELEMENTS = 384
CELLS = 8
PATCHES = 512
ROWS = 16
THIRDS = 3
QUARTERS = 4
WIDTH = 1920
WIDE_ROWS = 1216
BF = jnp.bfloat16
F32 = jnp.float32
VMEM_BYTES = 40 * 1024 * 1024
SOURCE_VMEM_BYTES = 60 * 1024 * 1024


def iota(shape, dim):
    return lax.broadcasted_iota(jnp.int32, shape, dim)


def dot(a, b):
    return jnp.dot(a, b, preferred_element_type=F32)


def dot_nt(a, b):
    return lax.dot_general(a, b, (((1,), (1,)), ((), ())), preferred_element_type=F32)


def one_hot(mask):
    return jnp.where(mask, 1.0, 0.0).astype(BF)


def turn(value, shift):
    return pltpu.roll(value, shift, 2)


def pack(out_ref, at, firsts, last):
    for h in range(THIRDS):
        block = firsts[h]
        for a in range(QUARTERS):
            lanes = slice(128 * (3 * a + h), 128 * (3 * a + h) + 128)
            out_ref[at, :, lanes] = block[:, 4 * a : 4 * a + 4, :].astype(BF)
    n = last.shape[0]
    front = iota((n, 4, 128), 2) < 96
    for i in range(THIRDS):
        tail = turn(last, 96 - 32 * i)[:, 12:16, :]
        lanes = slice(128 * (12 + i), 128 * (12 + i) + 128)
        out_ref[at, :, lanes] = jnp.where(front, last[:, 4 * i : 4 * i + 4, :], tail).astype(BF)


def unpack(ref, at, h):
    parts = []
    for a in range(QUARTERS):
        lanes = slice(128 * (3 * a + h), 128 * (3 * a + h) + 128)
        parts.append(ref[at, :, lanes].astype(F32))
    return jnp.concatenate(parts, axis=1)


def unpack_last(ref, at):
    tiles = [ref[at, :, 128 * (12 + i) : 128 * (12 + i) + 128].astype(F32) for i in range(THIRDS)]
    lane = iota(tiles[0].shape, 2) // 32
    tail = turn(tiles[0], 32)
    for h in range(1, THIRDS):
        tail = jnp.where(lane == h, turn(tiles[h], 32 * h + 32), tail)
    return jnp.concatenate(tiles + [tail], axis=1)


def place_of(group, k):
    return k % MEMBERS * CHANNELS + 2 * group + k // MEMBERS


def source_kernel(mem_ref, *refs):
    ens_hbm, small, (out_hbm, spread_hbm), landed = refs[0], refs[1:5], refs[5:7], refs[8:12]
    ens_ref, wide_ref, out_ref, spread_ref, side_ref, in_sems, out_sems = refs[7], *refs[12:18]
    fetches = [pltpu.make_async_copy(a, b, in_sems.at[k]) for k, (a, b) in enumerate(zip(small, landed))]
    members = [
        pltpu.make_async_copy(ens_hbm.at[m], ens_ref.at[m], in_sems.at[4 + m]) for m in range(MEMBERS)
    ]
    for copy in fetches + members:
        copy.start()
    for copy in fetches:
        copy.wait()
    margin_ref, owner_ref, patch_ref, letkf_ref = landed
    lane24 = iota((24, ELEMENTS), 1)
    block_of = (lane24 // 128) * 8 + lane24 % 8
    pick_block = iota((24, ELEMENTS), 0) == block_of
    expanded = dot(margin_ref[...], one_hot(pick_block))
    row = iota((256, ELEMENTS), 0)
    lane = iota((256, ELEMENTS), 1)
    fits = (row // 128 == (lane % 16) // 8) & (row % 8 == (lane % 128) // 16)
    expanded = jnp.where(fits, expanded, 0.0).astype(BF)
    fold = one_hot((iota((ELEMENTS, 256), 1) % 128) // 8 == iota((ELEMENTS, 256), 0) % 16)
    spread = dot(fold, expanded)
    er = iota((ELEMENTS, ELEMENTS), 0)
    el = iota((ELEMENTS, ELEMENTS), 1)
    spread = jnp.where(er // 16 == (el // 128) * 8 + el % 8, spread, 0.0)
    sums = jnp.sum(spread, axis=0, keepdims=True)
    spread = spread.astype(BF)
    spread_ref[...] = spread
    leaving = pltpu.make_async_copy(spread_ref, spread_hbm, out_sems.at[8])
    leaving.start()
    high = sums.astype(BF).astype(F32)
    low = sums - high

    dest = owner_ref[...] * 8 + patch_ref[...] - 256
    dest = dest.astype(F32).astype(BF)
    place = dot(dest, one_hot(pick_block))
    lane2 = iota((2, ELEMENTS), 1)
    place = jnp.sum(jnp.where((lane2 % 16) // 8 == iota((2, ELEMENTS), 0), place, 0.0), axis=0, keepdims=True)

    own = mem_ref[0] * MEMBERS
    pick_own = one_hot((iota((16, 40), 1) == own + iota((16, 40), 0)) & (iota((16, 40), 0) < MEMBERS))
    mine = dot_nt(pick_own, letkf_ref[...].astype(BF)).astype(BF)
    lane40 = iota((40, ELEMENTS), 1)
    weights = dot(mine, one_hot(iota((40, ELEMENTS), 0) == (lane40 // 128) * 16 + lane40 % 16))
    sides = [place, high, low] + [weights[n : n + 1] for n in range(MEMBERS)]
    side_ref[...] = jnp.concatenate(sides + [jnp.zeros((8, ELEMENTS), F32)], axis=0)
    spare = iota((16, 128), 0) == 15

    for m in range(MEMBERS):
        members[m].wait()
        pieces = dot(ens_ref[m], spread)
        for j in range(THIRDS):
            wide_ref[j, m * CHANNELS : (m + 1) * CHANNELS, :] = pieces[:, 128 * j : 128 * j + 128]

    def group_copy(group):
        part = pl.ds(8 * group, 8)
        return pltpu.make_async_copy(out_ref.at[part], out_hbm.at[part], out_sems.at[group])

    def send(group, carry):
        firsts, rest = [], []
        for h in range(THIRDS):
            lanes = slice(128 * h, 128 * h + 128)
            rows = []
            for k in range(2 * MEMBERS):
                tile = wide_ref[h, pl.ds(place_of(group, k), 16, 16), :]
                rows.append(jnp.where(spare, side_ref[k : k + 1, lanes], tile))
            firsts.append(jnp.concatenate(rows[:8], axis=0).T.reshape(8, ROWS, 128))
            rest += rows[8:]
        rest = jnp.concatenate(rest + [jnp.zeros((32, 128), F32)], axis=0)
        pack(out_ref, pl.ds(8 * group, 8), firsts, rest.T.reshape(8, ROWS, 128))
        group_copy(group).start()
        return carry

    lax.fori_loop(0, 8, send, 0)
    leaving.wait()
    for group in range(8):
        group_copy(group).wait()


def hits(first):
    place = first[:, 15:16] + 256.0
    lanes = iota((MESH * ROWS, PATCHES), 1).astype(F32)
    return one_hot(lanes == place)


def patch_kernel(got_ref, out_ref):
    every = slice(0, MESH)
    last_t = unpack_last(got_ref, every).reshape(MESH * ROWS, 128).T
    grid = jnp.zeros((160, PATCHES), F32)
    weights = [[None] * THIRDS for _ in range(MEMBERS)]
    for h in range(THIRDS):
        first = unpack(got_ref, every, h).reshape(MESH * ROWS, 128)
        first_t = first.T
        left = jnp.concatenate([first_t, last_t[32 * h : 32 * h + 32]], axis=0).astype(BF)
        grid = grid + dot(left, hits(first))
        for n in range(MEMBERS):
            weights[n][h] = first_t[63 + 16 * n : 64 + 16 * n]
    cover = grid[31:32] + grid[47:48]
    weights = sum(weights, []) + [jnp.zeros((1, MESH * ROWS), F32)]
    weights = jnp.concatenate(weights, axis=0).astype(BF)
    cover = jnp.maximum(cover, 1.0)
    grid = grid / cover
    for q in range(MEM):
        at = slice(64 * q, 64 * q + 64)
        out_ref[q, 0:80, :] = jnp.concatenate([grid[0:80, at], grid[80:160, at]], axis=1).astype(BF)
        out_ref[q, 80:96, :] = weights[:, 128 * q : 128 * q + 128]


def mixing_kernel(got_ref, out_ref, weight_ref, field_ref):
    tile = one_hot(iota((128, 128), 0) // 16 == (iota((128, 128), 1) % 64) // 8)
    lane = iota((ROWS, 128), 1)
    for q in range(MEM):
        wide = got_ref[q, 80:96, :]
        rows = [jnp.where(lane % 16 == r, wide, jnp.zeros_like(wide)) for r in range(ROWS)]
        weight_ref[q] = dot(jnp.concatenate(rows, axis=0), tile)
        field_ref[q] = got_ref[q, 0:80, :].astype(F32)

    def mix(q, carry):
        mixed = [jnp.zeros((16, 128), F32) for _ in range(MEMBERS)]
        for m in range(MEM * MEMBERS):
            row = (m % MEMBERS) * 16
            field = field_ref[m // MEMBERS, row : row + 16, :]
            for n in range(MEMBERS):
                w = (m % 16) * 16 + n * 3 + m // 16
                mixed[n] = mixed[n] + weight_ref[q, w : w + 1, :] * field
        for n in range(MEMBERS):
            out_ref[q, 16 * n : 16 * n + 16, :] = (mixed[n] - field_ref[q, 16 * n : 16 * n + 16, :]).astype(BF)
        return carry

    lax.fori_loop(0, MEM, mix, 0)


def expand_kernel(inc_ref, got_ref, out_ref):
    halves = [[], []]
    for q in range(0, MEM, 2):
        even, odd = inc_ref[q].astype(F32), inc_ref[q + 1].astype(F32)
        halves[0].append(jnp.concatenate([even[:, 0:64], odd[:, 0:64]], axis=1))
        halves[1].append(jnp.concatenate([even[:, 64:128], odd[:, 64:128]], axis=1))
    inc = jnp.concatenate([jnp.concatenate(half, axis=1) for half in halves], axis=0)
    first = inc[0:128].T.astype(BF)
    small = inc[128:160]
    last = jnp.zeros((MESH * ROWS, 128), F32)
    every = slice(0, MESH)
    firsts = []
    for h in range(THIRDS):
        pad = [jnp.zeros((32, PATCHES), F32)] * 4
        pad[h] = small
        right = jnp.concatenate([first, jnp.concatenate(pad, axis=0).T.astype(BF)], axis=1)
        back = dot(hits(unpack(got_ref, every, h).reshape(MESH * ROWS, 128)), right)
        firsts.append(back[:, 0:128].reshape(MESH, ROWS, 128))
        last = last + back[:, 128:256]
    pack(out_ref, every, firsts, last.reshape(MESH, ROWS, 128))


def final_kernel(back_ref, ens_ref, spread_ref, out_hbm, wide_ref, out_ref, sems):
    spread = spread_ref[...]
    area = dot_nt(jnp.ones((16, ELEMENTS), BF), spread)[0:1]
    scale = 1.0 / area

    def correct(group, carry):
        at = pl.ds(8 * group, 8)
        first = jnp.concatenate([unpack(back_ref, at, h).reshape(128, 128).T for h in range(THIRDS)], axis=1)
        last = unpack_last(back_ref, at).reshape(128, 128).T
        last = jnp.concatenate([last[32 * h : 32 * h + 32] for h in range(THIRDS)], axis=1)
        left = jnp.concatenate([first, last], axis=0).astype(BF)
        correction = dot_nt(left, spread) * scale
        for k in range(2 * MEMBERS):
            for j in range(3):
                wide_ref[j, pl.ds(place_of(group, k), 15, 16), :] = correction[
                    16 * k : 16 * k + 15, 128 * j : 128 * j + 128
                ]
        return carry

    lax.fori_loop(0, 8, correct, 0)
    copies = []
    for m in range(MEMBERS):
        for j in range(3):
            rows = slice(m * CHANNELS, (m + 1) * CHANNELS)
            lanes = slice(128 * j, 128 * j + 128)
            out_ref[m, :, lanes] = (ens_ref[m, :, lanes].astype(F32) + wide_ref[j, rows, :]).astype(BF)
        copies.append(pltpu.make_async_copy(out_ref.at[m], out_hbm.at[m], sems.at[m]))
        copies[-1].start()
    for copy in copies:
        copy.wait()


def vmem():
    return pl.BlockSpec(memory_space=pltpu.VMEM)


def hbm():
    return pl.BlockSpec(memory_space=pltpu.HBM)


def call(kernel, outs, ins, scratch=(), limit=VMEM_BYTES, place=vmem):
    return pl.pallas_call(
        kernel,
        out_shape=[jax.ShapeDtypeStruct(s, d) for s, d in outs],
        in_specs=ins,
        out_specs=[place() for _ in outs],
        scratch_shapes=list(scratch),
        compiler_params=pltpu.CompilerParams(vmem_limit_bytes=limit),
    )


def shards(ensemble, ovl_owner, ovl_patch, ovl_weight, letkf_weight):
    margin = ovl_weight.transpose(1, 2, 3, 0).reshape(256, 24)
    mem = lax.axis_index("mem").astype(jnp.int32).reshape(1)
    send, spread = call(
        source_kernel,
        [((MESH, QUARTERS, WIDTH), BF), ((ELEMENTS, ELEMENTS), BF)],
        [pl.BlockSpec(memory_space=pltpu.SMEM)] + [hbm()] * 5,
        [
            pltpu.VMEM((MEMBERS, CHANNELS, ELEMENTS), BF),
            pltpu.VMEM((256, 24), BF),
            pltpu.VMEM((2, 24), jnp.int32),
            pltpu.VMEM((2, 24), jnp.int32),
            pltpu.VMEM((MEM * MEMBERS, MEM * MEMBERS), F32),
            pltpu.VMEM((3, WIDE_ROWS, 128), F32),
            pltpu.VMEM((MESH, QUARTERS, WIDTH), BF),
            pltpu.VMEM((ELEMENTS, ELEMENTS), BF),
            pltpu.VMEM((16, ELEMENTS), F32),
            pltpu.SemaphoreType.DMA((9,)),
            pltpu.SemaphoreType.DMA((9,)),
        ],
        SOURCE_VMEM_BYTES,
        hbm,
    )(mem, ensemble, margin, ovl_owner.T, ovl_patch.T, letkf_weight[0])
    got = lax.all_to_all(send, "mesh", split_axis=0, concat_axis=0, tiled=True)
    (fields,) = call(patch_kernel, [((MEM, 96, 128), BF)], [vmem()])(got)
    fields = lax.all_to_all(fields, "mem", split_axis=0, concat_axis=0, tiled=True)
    (mixed,) = call(
        mixing_kernel,
        [((MEM, 80, 128), BF)],
        [vmem()],
        [pltpu.VMEM((MEM, 256, 128), F32), pltpu.VMEM((MEM, 80, 128), F32)],
    )(fields)
    mixed = lax.all_to_all(mixed, "mem", split_axis=0, concat_axis=0, tiled=True)
    (back,) = call(expand_kernel, [((MESH, QUARTERS, WIDTH), BF)], [vmem()] * 2)(mixed, got)
    returned = lax.all_to_all(back, "mesh", split_axis=0, concat_axis=0, tiled=True)
    (analysis,) = call(
        final_kernel,
        [((MEMBERS, CHANNELS, ELEMENTS), BF)],
        [vmem()] * 3,
        [
            pltpu.VMEM((3, WIDE_ROWS, 128), F32),
            pltpu.VMEM((MEMBERS, CHANNELS, ELEMENTS), BF),
            pltpu.SemaphoreType.DMA((MEMBERS,)),
        ],
        place=hbm,
    )(returned, ensemble, spread)
    return analysis


def solution(mesh):
    in_specs = (
        P("mem", None, "mesh"),
        P("mesh", None),
        P("mesh", None),
        P("mesh", None, None, None),
        P("mesh", None, None),
    )
    out_specs = P("mem", None, "mesh")
    return jax.shard_map(shards, mesh=mesh, in_specs=in_specs, out_specs=out_specs, check_vma=False)
```

```python
import jax
import jax.numpy as jnp
from jax import lax
from jax.experimental import pallas as pl
from jax.experimental.pallas import tpu as pltpu
from jax.sharding import PartitionSpec as P

MESH = 64
MEM = 8
MEMBERS = 5
CHANNELS = 240
ELEMENTS = 384
CELLS = 8
PATCHES = 512
ROWS = 16
THIRDS = 3
QUARTERS = 4
WIDTH = 1920
WIDE_ROWS = 1216
BF = jnp.bfloat16
F32 = jnp.float32
VMEM_BYTES = 40 * 1024 * 1024
SOURCE_VMEM_BYTES = 60 * 1024 * 1024


def iota(shape, dim):
    return lax.broadcasted_iota(jnp.int32, shape, dim)


def dot(a, b):
    return jnp.dot(a, b, preferred_element_type=F32)


def dot_nt(a, b):
    return lax.dot_general(a, b, (((1,), (1,)), ((), ())), preferred_element_type=F32)


def one_hot(mask):
    return jnp.where(mask, 1.0, 0.0).astype(BF)


def turn(value, shift):
    return pltpu.roll(value, shift, 2)


def pack(out_ref, at, firsts, last):
    for h in range(THIRDS):
        block = firsts[h]
        for a in range(QUARTERS):
            lanes = slice(128 * (3 * a + h), 128 * (3 * a + h) + 128)
            out_ref[at, :, lanes] = block[:, 4 * a : 4 * a + 4, :].astype(BF)
    n = last.shape[0]
    front = iota((n, 4, 128), 2) < 96
    for i in range(THIRDS):
        tail = turn(last, 96 - 32 * i)[:, 12:16, :]
        lanes = slice(128 * (12 + i), 128 * (12 + i) + 128)
        out_ref[at, :, lanes] = jnp.where(front, last[:, 4 * i : 4 * i + 4, :], tail).astype(BF)


def unpack(ref, at, h):
    parts = []
    for a in range(QUARTERS):
        lanes = slice(128 * (3 * a + h), 128 * (3 * a + h) + 128)
        parts.append(ref[at, :, lanes].astype(F32))
    return jnp.concatenate(parts, axis=1)


def unpack_last(ref, at):
    tiles = [ref[at, :, 128 * (12 + i) : 128 * (12 + i) + 128].astype(F32) for i in range(THIRDS)]
    lane = iota(tiles[0].shape, 2) // 32
    tail = turn(tiles[0], 32)
    for h in range(1, THIRDS):
        tail = jnp.where(lane == h, turn(tiles[h], 32 * h + 32), tail)
    return jnp.concatenate(tiles + [tail], axis=1)


def place_of(group, k):
    return k % MEMBERS * CHANNELS + 2 * group + k // MEMBERS


def source_kernel(mem_ref, *refs):
    ens_hbm, small, (out_hbm, spread_hbm), landed = refs[0], refs[1:5], refs[5:7], refs[8:12]
    ens_ref, wide_ref, out_ref, spread_ref, side_ref, in_sems, out_sems = refs[7], *refs[12:18]
    fetches = [pltpu.make_async_copy(a, b, in_sems.at[k]) for k, (a, b) in enumerate(zip(small, landed))]
    members = [
        pltpu.make_async_copy(ens_hbm.at[m], ens_ref.at[m], in_sems.at[4 + m]) for m in range(MEMBERS)
    ]
    for copy in fetches + members:
        copy.start()
    for copy in fetches:
        copy.wait()
    margin_ref, owner_ref, patch_ref, letkf_ref = landed
    lane24 = iota((24, ELEMENTS), 1)
    block_of = (lane24 // 128) * 8 + lane24 % 8
    pick_block = iota((24, ELEMENTS), 0) == block_of
    expanded = dot(margin_ref[...], one_hot(pick_block))
    row = iota((256, ELEMENTS), 0)
    lane = iota((256, ELEMENTS), 1)
    fits = (row // 128 == (lane % 16) // 8) & (row % 8 == (lane % 128) // 16)
    expanded = jnp.where(fits, expanded, 0.0).astype(BF)
    fold = one_hot((iota((ELEMENTS, 256), 1) % 128) // 8 == iota((ELEMENTS, 256), 0) % 16)
    spread = dot(fold, expanded)
    er = iota((ELEMENTS, ELEMENTS), 0)
    el = iota((ELEMENTS, ELEMENTS), 1)
    spread = jnp.where(er // 16 == (el // 128) * 8 + el % 8, spread, 0.0)
    sums = jnp.sum(spread, axis=0, keepdims=True)
    spread = spread.astype(BF)
    spread_ref[...] = spread
    leaving = [pltpu.make_async_copy(spread_ref, spread_hbm, out_sems.at[8])]
    leaving[0].start()
    high = sums.astype(BF).astype(F32)
    low = sums - high

    dest = owner_ref[...] * 8 + patch_ref[...] - 256
    dest = dest.astype(F32).astype(BF)
    place = dot(dest, one_hot(pick_block))
    lane2 = iota((2, ELEMENTS), 1)
    place = jnp.sum(jnp.where((lane2 % 16) // 8 == iota((2, ELEMENTS), 0), place, 0.0), axis=0, keepdims=True)

    own = mem_ref[0] * MEMBERS
    pick_own = one_hot((iota((16, 40), 1) == own + iota((16, 40), 0)) & (iota((16, 40), 0) < MEMBERS))
    mine = dot_nt(pick_own, letkf_ref[...].astype(BF)).astype(BF)
    lane40 = iota((40, ELEMENTS), 1)
    weights = dot(mine, one_hot(iota((40, ELEMENTS), 0) == (lane40 // 128) * 16 + lane40 % 16))
    sides = [place, high, low] + [weights[n : n + 1] for n in range(MEMBERS)]
    side_ref[...] = jnp.concatenate(sides + [jnp.zeros((8, ELEMENTS), F32)], axis=0)
    spare = iota((16, 128), 0) == 15

    for m in range(MEMBERS):
        members[m].wait()
        pieces = dot(ens_ref[m], spread)
        for j in range(THIRDS):
            wide_ref[j, m * CHANNELS : (m + 1) * CHANNELS, :] = pieces[:, 128 * j : 128 * j + 128]

    for group in range(8):
        firsts, rest = [], []
        for h in range(THIRDS):
            lanes = slice(128 * h, 128 * h + 128)
            rows = []
            for k in range(2 * MEMBERS):
                tile = wide_ref[h, pl.ds(place_of(group, k), 16, 16), :]
                rows.append(jnp.where(spare, side_ref[k : k + 1, lanes], tile))
            firsts.append(jnp.concatenate(rows[:8], axis=0).T.reshape(8, ROWS, 128))
            rest += rows[8:]
        rest = jnp.concatenate(rest + [jnp.zeros((32, 128), F32)], axis=0)
        pack(out_ref, pl.ds(8 * group, 8), firsts, rest.T.reshape(8, ROWS, 128))
        part = pl.ds(8 * group, 8)
        leaving.append(pltpu.make_async_copy(out_ref.at[part], out_hbm.at[part], out_sems.at[group]))
        leaving[-1].start()
    for copy in leaving:
        copy.wait()


def hits(first):
    place = first[:, 15:16] + 256.0
    lanes = iota((MESH * ROWS, PATCHES), 1).astype(F32)
    return one_hot(lanes == place)


def patch_kernel(got_ref, out_ref):
    every = slice(0, MESH)
    last_t = unpack_last(got_ref, every).reshape(MESH * ROWS, 128).T
    grid = jnp.zeros((160, PATCHES), F32)
    weights = [[None] * THIRDS for _ in range(MEMBERS)]
    for h in range(THIRDS):
        first = unpack(got_ref, every, h).reshape(MESH * ROWS, 128)
        first_t = first.T
        left = jnp.concatenate([first_t, last_t[32 * h : 32 * h + 32]], axis=0).astype(BF)
        grid = grid + dot(left, hits(first))
        for n in range(MEMBERS):
            weights[n][h] = first_t[63 + 16 * n : 64 + 16 * n]
    cover = grid[31:32] + grid[47:48]
    weights = sum(weights, []) + [jnp.zeros((1, MESH * ROWS), F32)]
    weights = jnp.concatenate(weights, axis=0).astype(BF)
    cover = jnp.maximum(cover, 1.0)
    grid = grid / cover
    for q in range(MEM):
        at = slice(64 * q, 64 * q + 64)
        out_ref[q, 0:80, :] = jnp.concatenate([grid[0:80, at], grid[80:160, at]], axis=1).astype(BF)
        out_ref[q, 80:96, :] = weights[:, 128 * q : 128 * q + 128]


def mixing_kernel(got_ref, out_ref, weight_ref, field_ref):
    tile = one_hot(iota((128, 128), 0) // 16 == (iota((128, 128), 1) % 64) // 8)
    lane = iota((ROWS, 128), 1)
    for q in range(MEM):
        wide = got_ref[q, 80:96, :]
        rows = [jnp.where(lane % 16 == r, wide, jnp.zeros_like(wide)) for r in range(ROWS)]
        weight_ref[q] = dot(jnp.concatenate(rows, axis=0), tile)
        field_ref[q] = got_ref[q, 0:80, :].astype(F32)

    def mix(q, carry):
        mixed = [jnp.zeros((16, 128), F32) for _ in range(MEMBERS)]
        for m in range(MEM * MEMBERS):
            row = (m % MEMBERS) * 16
            field = field_ref[m // MEMBERS, row : row + 16, :]
            for n in range(MEMBERS):
                w = (m % 16) * 16 + n * 3 + m // 16
                mixed[n] = mixed[n] + weight_ref[q, w : w + 1, :] * field
        for n in range(MEMBERS):
            out_ref[q, 16 * n : 16 * n + 16, :] = (mixed[n] - field_ref[q, 16 * n : 16 * n + 16, :]).astype(BF)
        return carry

    lax.fori_loop(0, MEM, mix, 0)


def expand_kernel(inc_ref, got_ref, out_ref):
    halves = [[], []]
    for q in range(0, MEM, 2):
        even, odd = inc_ref[q].astype(F32), inc_ref[q + 1].astype(F32)
        halves[0].append(jnp.concatenate([even[:, 0:64], odd[:, 0:64]], axis=1))
        halves[1].append(jnp.concatenate([even[:, 64:128], odd[:, 64:128]], axis=1))
    inc = jnp.concatenate([jnp.concatenate(half, axis=1) for half in halves], axis=0)
    first = inc[0:128].T.astype(BF)
    small = inc[128:160]
    last = jnp.zeros((MESH * ROWS, 128), F32)
    every = slice(0, MESH)
    firsts = []
    for h in range(THIRDS):
        pad = [jnp.zeros((32, PATCHES), F32)] * 4
        pad[h] = small
        right = jnp.concatenate([first, jnp.concatenate(pad, axis=0).T.astype(BF)], axis=1)
        back = dot(hits(unpack(got_ref, every, h).reshape(MESH * ROWS, 128)), right)
        firsts.append(back[:, 0:128].reshape(MESH, ROWS, 128))
        last = last + back[:, 128:256]
    pack(out_ref, every, firsts, last.reshape(MESH, ROWS, 128))


def final_kernel(back_ref, ens_ref, spread_ref, out_hbm, wide_ref, out_ref, sems):
    spread = spread_ref[...]
    area = dot_nt(jnp.ones((16, ELEMENTS), BF), spread)[0:1]
    scale = 1.0 / area
    for group in range(8):
        at = slice(8 * group, 8 * group + 8)
        first = jnp.concatenate([unpack(back_ref, at, h).reshape(128, 128).T for h in range(THIRDS)], axis=1)
        last = unpack_last(back_ref, at).reshape(128, 128).T
        last = jnp.concatenate([last[32 * h : 32 * h + 32] for h in range(THIRDS)], axis=1)
        left = jnp.concatenate([first, last], axis=0).astype(BF)
        correction = dot_nt(left, spread) * scale
        for k in range(2 * MEMBERS):
            for j in range(3):
                wide_ref[j, pl.ds(place_of(group, k), 15, 16), :] = correction[
                    16 * k : 16 * k + 15, 128 * j : 128 * j + 128
                ]
    copies = []
    for m in range(MEMBERS):
        for j in range(3):
            rows = slice(m * CHANNELS, (m + 1) * CHANNELS)
            lanes = slice(128 * j, 128 * j + 128)
            out_ref[m, :, lanes] = (ens_ref[m, :, lanes].astype(F32) + wide_ref[j, rows, :]).astype(BF)
        copies.append(pltpu.make_async_copy(out_ref.at[m], out_hbm.at[m], sems.at[m]))
        copies[-1].start()
    for copy in copies:
        copy.wait()


def vmem():
    return pl.BlockSpec(memory_space=pltpu.VMEM)


def hbm():
    return pl.BlockSpec(memory_space=pltpu.HBM)


def call(kernel, outs, ins, scratch=(), limit=VMEM_BYTES, place=vmem):
    return pl.pallas_call(
        kernel,
        out_shape=[jax.ShapeDtypeStruct(s, d) for s, d in outs],
        in_specs=ins,
        out_specs=[place() for _ in outs],
        scratch_shapes=list(scratch),
        compiler_params=pltpu.CompilerParams(vmem_limit_bytes=limit),
    )


def shards(ensemble, ovl_owner, ovl_patch, ovl_weight, letkf_weight):
    margin = ovl_weight.transpose(1, 2, 3, 0).reshape(256, 24)
    mem = lax.axis_index("mem").astype(jnp.int32).reshape(1)
    send, spread = call(
        source_kernel,
        [((MESH, QUARTERS, WIDTH), BF), ((ELEMENTS, ELEMENTS), BF)],
        [pl.BlockSpec(memory_space=pltpu.SMEM)] + [hbm()] * 5,
        [
            pltpu.VMEM((MEMBERS, CHANNELS, ELEMENTS), BF),
            pltpu.VMEM((256, 24), BF),
            pltpu.VMEM((2, 24), jnp.int32),
            pltpu.VMEM((2, 24), jnp.int32),
            pltpu.VMEM((MEM * MEMBERS, MEM * MEMBERS), F32),
            pltpu.VMEM((3, WIDE_ROWS, 128), F32),
            pltpu.VMEM((MESH, QUARTERS, WIDTH), BF),
            pltpu.VMEM((ELEMENTS, ELEMENTS), BF),
            pltpu.VMEM((16, ELEMENTS), F32),
            pltpu.SemaphoreType.DMA((9,)),
            pltpu.SemaphoreType.DMA((9,)),
        ],
        SOURCE_VMEM_BYTES,
        hbm,
    )(mem, ensemble, margin, ovl_owner.T, ovl_patch.T, letkf_weight[0])
    got = lax.all_to_all(send, "mesh", split_axis=0, concat_axis=0, tiled=True)
    (fields,) = call(patch_kernel, [((MEM, 96, 128), BF)], [vmem()])(got)
    fields = lax.all_to_all(fields, "mem", split_axis=0, concat_axis=0, tiled=True)
    (mixed,) = call(
        mixing_kernel,
        [((MEM, 80, 128), BF)],
        [vmem()],
        [pltpu.VMEM((MEM, 256, 128), F32), pltpu.VMEM((MEM, 80, 128), F32)],
    )(fields)
    mixed = lax.all_to_all(mixed, "mem", split_axis=0, concat_axis=0, tiled=True)
    (back,) = call(expand_kernel, [((MESH, QUARTERS, WIDTH), BF)], [vmem()] * 2)(mixed, got)
    returned = lax.all_to_all(back, "mesh", split_axis=0, concat_axis=0, tiled=True)
    (analysis,) = call(
        final_kernel,
        [((MEMBERS, CHANNELS, ELEMENTS), BF)],
        [vmem()] * 3,
        [
            pltpu.VMEM((3, WIDE_ROWS, 128), F32),
            pltpu.VMEM((MEMBERS, CHANNELS, ELEMENTS), BF),
            pltpu.SemaphoreType.DMA((MEMBERS,)),
        ],
        place=hbm,
    )(returned, ensemble, spread)
    return analysis


def solution(mesh):
    in_specs = (
        P("mem", None, "mesh"),
        P("mesh", None),
        P("mesh", None),
        P("mesh", None, None, None),
        P("mesh", None, None),
    )
    out_specs = P("mem", None, "mesh")
    return jax.shard_map(shards, mesh=mesh, in_specs=in_specs, out_specs=out_specs, check_vma=False)
```

```python
import jax
import jax.numpy as jnp
from jax import lax
from jax.experimental import pallas as pl
from jax.experimental.pallas import tpu as pltpu
from jax.sharding import PartitionSpec as P

MESH = 64
MEM = 8
MEMBERS = 5
CHANNELS = 240
ELEMENTS = 384
CELLS = 8
PATCHES = 512
ROWS = 16
THIRDS = 3
QUARTERS = 4
WIDTH = 1920
WIDE_ROWS = 1216
BF = jnp.bfloat16
F32 = jnp.float32
VMEM_BYTES = 40 * 1024 * 1024
SOURCE_VMEM_BYTES = 60 * 1024 * 1024


def iota(shape, dim):
    return lax.broadcasted_iota(jnp.int32, shape, dim)


def dot(a, b):
    return jnp.dot(a, b, preferred_element_type=F32)


def dot_nt(a, b):
    return lax.dot_general(a, b, (((1,), (1,)), ((), ())), preferred_element_type=F32)


def one_hot(mask):
    return jnp.where(mask, 1.0, 0.0).astype(BF)


def turn(value, shift):
    return pltpu.roll(value, shift, 2)


def pack(out_ref, at, firsts, last):
    for h in range(THIRDS):
        block = firsts[h]
        for a in range(QUARTERS):
            lanes = slice(128 * (3 * a + h), 128 * (3 * a + h) + 128)
            out_ref[at, :, lanes] = block[:, 4 * a : 4 * a + 4, :].astype(BF)
    n = last.shape[0]
    front = iota((n, 4, 128), 2) < 96
    for i in range(THIRDS):
        tail = turn(last, 96 - 32 * i)[:, 12:16, :]
        lanes = slice(128 * (12 + i), 128 * (12 + i) + 128)
        out_ref[at, :, lanes] = jnp.where(front, last[:, 4 * i : 4 * i + 4, :], tail).astype(BF)


def unpack(ref, at, h):
    parts = []
    for a in range(QUARTERS):
        lanes = slice(128 * (3 * a + h), 128 * (3 * a + h) + 128)
        parts.append(ref[at, :, lanes].astype(F32))
    return jnp.concatenate(parts, axis=1)


def unpack_last(ref, at):
    tiles = [ref[at, :, 128 * (12 + i) : 128 * (12 + i) + 128].astype(F32) for i in range(THIRDS)]
    lane = iota(tiles[0].shape, 2) // 32
    tail = turn(tiles[0], 32)
    for h in range(1, THIRDS):
        tail = jnp.where(lane == h, turn(tiles[h], 32 * h + 32), tail)
    return jnp.concatenate(tiles + [tail], axis=1)


def places(group):
    return [m * CHANNELS + 2 * group + parity for parity in range(2) for m in range(MEMBERS)]


def source_kernel(mem_ref, *refs):
    ens_hbm, small, (out_hbm, spread_hbm), landed = refs[0], refs[1:5], refs[5:7], refs[8:12]
    ens_ref, wide_ref, out_ref, spread_ref, in_sems, out_sems = refs[7], *refs[12:17]
    fetches = [pltpu.make_async_copy(a, b, in_sems.at[k]) for k, (a, b) in enumerate(zip(small, landed))]
    members = [
        pltpu.make_async_copy(ens_hbm.at[m], ens_ref.at[m], in_sems.at[4 + m]) for m in range(MEMBERS)
    ]
    for copy in fetches + members:
        copy.start()
    for copy in fetches:
        copy.wait()
    margin_ref, owner_ref, patch_ref, letkf_ref = landed
    lane24 = iota((24, ELEMENTS), 1)
    block_of = (lane24 // 128) * 8 + lane24 % 8
    pick_block = iota((24, ELEMENTS), 0) == block_of
    expanded = dot(margin_ref[...], one_hot(pick_block))
    row = iota((256, ELEMENTS), 0)
    lane = iota((256, ELEMENTS), 1)
    fits = (row // 128 == (lane % 16) // 8) & (row % 8 == (lane % 128) // 16)
    expanded = jnp.where(fits, expanded, 0.0).astype(BF)
    fold = one_hot((iota((ELEMENTS, 256), 1) % 128) // 8 == iota((ELEMENTS, 256), 0) % 16)
    spread = dot(fold, expanded)
    er = iota((ELEMENTS, ELEMENTS), 0)
    el = iota((ELEMENTS, ELEMENTS), 1)
    spread = jnp.where(er // 16 == (el // 128) * 8 + el % 8, spread, 0.0)
    sums = jnp.sum(spread, axis=0, keepdims=True)
    spread = spread.astype(BF)
    spread_ref[...] = spread
    leaving = [pltpu.make_async_copy(spread_ref, spread_hbm, out_sems.at[8])]
    leaving[0].start()
    high = sums.astype(BF).astype(F32)
    low = sums - high

    dest = owner_ref[...] * 8 + patch_ref[...] - 256
    dest = dest.astype(F32).astype(BF)
    place = dot(dest, one_hot(pick_block))
    lane2 = iota((2, ELEMENTS), 1)
    place = jnp.sum(jnp.where((lane2 % 16) // 8 == iota((2, ELEMENTS), 0), place, 0.0), axis=0, keepdims=True)

    own = mem_ref[0] * MEMBERS
    pick_own = one_hot((iota((16, 40), 1) == own + iota((16, 40), 0)) & (iota((16, 40), 0) < MEMBERS))
    mine = dot_nt(pick_own, letkf_ref[...].astype(BF)).astype(BF)
    lane40 = iota((40, ELEMENTS), 1)
    weights = dot(mine, one_hot(iota((40, ELEMENTS), 0) == (lane40 // 128) * 16 + lane40 % 16))
    sides = [place, high, low] + [weights[n : n + 1] for n in range(MEMBERS)] + [jnp.zeros_like(low)] * 2
    spare = iota((16, ELEMENTS), 0) == 15

    for m in range(MEMBERS):
        members[m].wait()
        for j in range(3):
            rows = slice(m * CHANNELS, (m + 1) * CHANNELS)
            wide_ref[j, rows, :] = ens_ref[m, :, 128 * j : 128 * j + 128].astype(F32)
    tiles = [
        jnp.concatenate([wide_ref[j, pl.ds(start, 16, 16), :] for j in range(3)], axis=1)
        for group in range(8)
        for start in places(group)
    ]
    product = dot(jnp.concatenate(tiles, axis=0).astype(BF), spread)
    for group in range(8):
        pieces = product[160 * group : 160 * group + 160]
        pieces = jnp.concatenate(
            [jnp.where(spare, sides[k], pieces[16 * k : 16 * k + 16]) for k in range(10)], axis=0
        )
        firsts = [pieces[0:128, 128 * h : 128 * h + 128].astype(BF).T.reshape(8, ROWS, 128) for h in range(THIRDS)]
        rest = [pieces[128:160, 128 * h : 128 * h + 128] for h in range(THIRDS)]
        rest = jnp.concatenate(rest + [jnp.zeros((32, 128), F32)], axis=0)
        pack(out_ref, slice(8 * group, 8 * group + 8), firsts, rest.T.reshape(8, ROWS, 128))
        part = pl.ds(8 * group, 8)
        leaving.append(pltpu.make_async_copy(out_ref.at[part], out_hbm.at[part], out_sems.at[group]))
        leaving[-1].start()
    for copy in leaving:
        copy.wait()


def hits(first):
    place = first[:, 15:16] + 256.0
    lanes = iota((MESH * ROWS, PATCHES), 1).astype(F32)
    return one_hot(lanes == place)


def patch_kernel(got_ref, out_ref):
    every = slice(0, MESH)
    last_t = unpack_last(got_ref, every).reshape(MESH * ROWS, 128).T
    grid = jnp.zeros((160, PATCHES), F32)
    weights = [[None] * THIRDS for _ in range(MEMBERS)]
    for h in range(THIRDS):
        first = unpack(got_ref, every, h).reshape(MESH * ROWS, 128)
        first_t = first.T
        left = jnp.concatenate([first_t, last_t[32 * h : 32 * h + 32]], axis=0).astype(BF)
        grid = grid + dot(left, hits(first))
        for n in range(MEMBERS):
            weights[n][h] = first_t[63 + 16 * n : 64 + 16 * n]
    cover = grid[31:32] + grid[47:48]
    weights = sum(weights, []) + [jnp.zeros((1, MESH * ROWS), F32)]
    weights = jnp.concatenate(weights, axis=0).astype(BF)
    cover = jnp.maximum(cover, 1.0)
    grid = grid / cover
    for q in range(MEM):
        at = slice(64 * q, 64 * q + 64)
        out_ref[q, 0:80, :] = jnp.concatenate([grid[0:80, at], grid[80:160, at]], axis=1).astype(BF)
        out_ref[q, 80:96, :] = weights[:, 128 * q : 128 * q + 128]


def mixing_kernel(got_ref, out_ref, weight_ref, field_ref):
    tile = one_hot(iota((128, 128), 0) // 16 == (iota((128, 128), 1) % 64) // 8)
    lane = iota((ROWS, 128), 1)
    for q in range(MEM):
        wide = got_ref[q, 80:96, :]
        rows = [jnp.where(lane % 16 == r, wide, jnp.zeros_like(wide)) for r in range(ROWS)]
        weight_ref[q] = dot(jnp.concatenate(rows, axis=0), tile)
        field_ref[q] = got_ref[q, 0:80, :].astype(F32)

    def mix(q, carry):
        mixed = [jnp.zeros((16, 128), F32) for _ in range(MEMBERS)]
        for m in range(MEM * MEMBERS):
            row = (m % MEMBERS) * 16
            field = field_ref[m // MEMBERS, row : row + 16, :]
            for n in range(MEMBERS):
                w = (m % 16) * 16 + n * 3 + m // 16
                mixed[n] = mixed[n] + weight_ref[q, w : w + 1, :] * field
        for n in range(MEMBERS):
            out_ref[q, 16 * n : 16 * n + 16, :] = (mixed[n] - field_ref[q, 16 * n : 16 * n + 16, :]).astype(BF)

    for q in range(MEM):
        mix(q, 0)


def expand_kernel(inc_ref, got_ref, out_ref):
    halves = [[], []]
    for q in range(0, MEM, 2):
        even, odd = inc_ref[q].astype(F32), inc_ref[q + 1].astype(F32)
        halves[0].append(jnp.concatenate([even[:, 0:64], odd[:, 0:64]], axis=1))
        halves[1].append(jnp.concatenate([even[:, 64:128], odd[:, 64:128]], axis=1))
    inc = jnp.concatenate([jnp.concatenate(half, axis=1) for half in halves], axis=0)
    first = inc[0:128].T.astype(BF)
    small = inc[128:160]
    last = jnp.zeros((MESH * ROWS, 128), F32)
    every = slice(0, MESH)
    firsts = []
    for h in range(THIRDS):
        pad = [jnp.zeros((32, PATCHES), F32)] * 4
        pad[h] = small
        right = jnp.concatenate([first, jnp.concatenate(pad, axis=0).T.astype(BF)], axis=1)
        back = dot(hits(unpack(got_ref, every, h).reshape(MESH * ROWS, 128)), right)
        firsts.append(back[:, 0:128].reshape(MESH, ROWS, 128))
        last = last + back[:, 128:256]
    pack(out_ref, every, firsts, last.reshape(MESH, ROWS, 128))


def final_kernel(back_ref, ens_ref, spread_ref, out_hbm, wide_ref, out_ref, sems):
    spread = spread_ref[...]
    area = dot_nt(jnp.ones((16, ELEMENTS), BF), spread)[0:1]
    scale = 1.0 / area
    lefts = []
    for group in range(8):
        at = slice(8 * group, 8 * group + 8)
        first = jnp.concatenate([unpack(back_ref, at, h).reshape(128, 128).astype(BF).T for h in range(THIRDS)], axis=1)
        last = unpack_last(back_ref, at).reshape(128, 128).T
        last = jnp.concatenate([last[32 * h : 32 * h + 32] for h in range(THIRDS)], axis=1)
        lefts.append(jnp.concatenate([first, last.astype(BF)], axis=0))
    correction = dot_nt(jnp.concatenate(lefts, axis=0), spread) * scale
    copies = []
    for m in range(MEMBERS):
        for j in range(3):
            lanes = slice(128 * j, 128 * j + 128)
            for group in range(8):
                for parity in range(2):
                    row = 160 * group + 80 * parity + 16 * m
                    rows = pl.ds(m * CHANNELS + 2 * group + parity, 15, 16)
                    wide_ref[j, rows, :] = correction[row : row + 15, lanes]
            rows = slice(m * CHANNELS, (m + 1) * CHANNELS)
            out_ref[m, :, lanes] = (ens_ref[m, :, lanes].astype(F32) + wide_ref[j, rows, :]).astype(BF)
        copies.append(pltpu.make_async_copy(out_ref.at[m], out_hbm.at[m], sems.at[m]))
        copies[-1].start()
    for copy in copies:
        copy.wait()


def vmem():
    return pl.BlockSpec(memory_space=pltpu.VMEM)


def hbm():
    return pl.BlockSpec(memory_space=pltpu.HBM)


def call(kernel, outs, ins, scratch=(), limit=VMEM_BYTES, place=vmem):
    return pl.pallas_call(
        kernel,
        out_shape=[jax.ShapeDtypeStruct(s, d) for s, d in outs],
        in_specs=ins,
        out_specs=[place() for _ in outs],
        scratch_shapes=list(scratch),
        compiler_params=pltpu.CompilerParams(vmem_limit_bytes=limit),
    )


def shards(ensemble, ovl_owner, ovl_patch, ovl_weight, letkf_weight):
    margin = ovl_weight.transpose(1, 2, 3, 0).reshape(256, 24)
    mem = lax.axis_index("mem").astype(jnp.int32).reshape(1)
    send, spread = call(
        source_kernel,
        [((MESH, QUARTERS, WIDTH), BF), ((ELEMENTS, ELEMENTS), BF)],
        [pl.BlockSpec(memory_space=pltpu.SMEM)] + [hbm()] * 5,
        [
            pltpu.VMEM((MEMBERS, CHANNELS, ELEMENTS), BF),
            pltpu.VMEM((256, 24), BF),
            pltpu.VMEM((2, 24), jnp.int32),
            pltpu.VMEM((2, 24), jnp.int32),
            pltpu.VMEM((MEM * MEMBERS, MEM * MEMBERS), F32),
            pltpu.VMEM((3, WIDE_ROWS, 128), F32),
            pltpu.VMEM((MESH, QUARTERS, WIDTH), BF),
            pltpu.VMEM((ELEMENTS, ELEMENTS), BF),
            pltpu.SemaphoreType.DMA((9,)),
            pltpu.SemaphoreType.DMA((9,)),
        ],
        SOURCE_VMEM_BYTES,
        hbm,
    )(mem, ensemble, margin, ovl_owner.T, ovl_patch.T, letkf_weight[0])
    got = lax.all_to_all(send, "mesh", split_axis=0, concat_axis=0, tiled=True)
    (fields,) = call(patch_kernel, [((MEM, 96, 128), BF)], [vmem()])(got)
    fields = lax.all_to_all(fields, "mem", split_axis=0, concat_axis=0, tiled=True)
    (mixed,) = call(
        mixing_kernel,
        [((MEM, 80, 128), BF)],
        [vmem()],
        [pltpu.VMEM((MEM, 256, 128), F32), pltpu.VMEM((MEM, 80, 128), F32)],
    )(fields)
    mixed = lax.all_to_all(mixed, "mem", split_axis=0, concat_axis=0, tiled=True)
    (back,) = call(expand_kernel, [((MESH, QUARTERS, WIDTH), BF)], [vmem()] * 2)(mixed, got)
    returned = lax.all_to_all(back, "mesh", split_axis=0, concat_axis=0, tiled=True)
    (analysis,) = call(
        final_kernel,
        [((MEMBERS, CHANNELS, ELEMENTS), BF)],
        [vmem()] * 3,
        [
            pltpu.VMEM((3, WIDE_ROWS, 128), F32),
            pltpu.VMEM((MEMBERS, CHANNELS, ELEMENTS), BF),
            pltpu.SemaphoreType.DMA((MEMBERS,)),
        ],
        place=hbm,
    )(returned, ensemble, spread)
    return analysis


def solution(mesh):
    in_specs = (
        P("mem", None, "mesh"),
        P("mesh", None),
        P("mesh", None),
        P("mesh", None, None, None),
        P("mesh", None, None),
    )
    out_specs = P("mem", None, "mesh")
    return jax.shard_map(shards, mesh=mesh, in_specs=in_specs, out_specs=out_specs, check_vma=False)
```

```python
import jax
import jax.numpy as jnp
from jax import lax
from jax.experimental import pallas as pl
from jax.experimental.pallas import tpu as pltpu
from jax.sharding import PartitionSpec as P

MESH = 64
MEM = 8
MEMBERS = 5
CHANNELS = 240
ELEMENTS = 384
CELLS = 8
PATCHES = 512
ROWS = 16
THIRDS = 3
QUARTERS = 4
WIDTH = 1920
WIDE_ROWS = 1216
BF = jnp.bfloat16
F32 = jnp.float32
VMEM_BYTES = 40 * 1024 * 1024
SOURCE_VMEM_BYTES = 60 * 1024 * 1024


def iota(shape, dim):
    return lax.broadcasted_iota(jnp.int32, shape, dim)


def dot(a, b):
    return jnp.dot(a, b, preferred_element_type=F32)


def dot_nt(a, b):
    return lax.dot_general(a, b, (((1,), (1,)), ((), ())), preferred_element_type=F32)


def one_hot(mask):
    return jnp.where(mask, 1.0, 0.0).astype(BF)


def turn(value, shift):
    return pltpu.roll(value, shift, 2)


def pack(out_ref, at, firsts, last):
    for h in range(THIRDS):
        block = firsts[h]
        for a in range(QUARTERS):
            lanes = slice(128 * (3 * a + h), 128 * (3 * a + h) + 128)
            out_ref[at, :, lanes] = block[:, 4 * a : 4 * a + 4, :].astype(BF)
    n = last.shape[0]
    front = iota((n, 4, 128), 2) < 96
    for i in range(THIRDS):
        tail = turn(last, 96 - 32 * i)[:, 12:16, :]
        lanes = slice(128 * (12 + i), 128 * (12 + i) + 128)
        out_ref[at, :, lanes] = jnp.where(front, last[:, 4 * i : 4 * i + 4, :], tail).astype(BF)


def unpack(ref, at, h):
    parts = []
    for a in range(QUARTERS):
        lanes = slice(128 * (3 * a + h), 128 * (3 * a + h) + 128)
        parts.append(ref[at, :, lanes].astype(F32))
    return jnp.concatenate(parts, axis=1)


def unpack_last(ref, at):
    tiles = [ref[at, :, 128 * (12 + i) : 128 * (12 + i) + 128].astype(F32) for i in range(THIRDS)]
    lane = iota(tiles[0].shape, 2) // 32
    tail = turn(tiles[0], 32)
    for h in range(1, THIRDS):
        tail = jnp.where(lane == h, turn(tiles[h], 32 * h + 32), tail)
    return jnp.concatenate(tiles + [tail], axis=1)


def places(group):
    return [m * CHANNELS + 2 * group + parity for parity in range(2) for m in range(MEMBERS)]


def source_kernel(mem_ref, *refs):
    ens_hbm, small, (out_hbm, spread_hbm), landed = refs[0], refs[1:5], refs[5:7], refs[8:12]
    ens_ref, wide_ref, out_ref, spread_ref, in_sems, out_sems = refs[7], *refs[12:17]
    fetches = [pltpu.make_async_copy(a, b, in_sems.at[k]) for k, (a, b) in enumerate(zip(small, landed))]
    members = [
        pltpu.make_async_copy(ens_hbm.at[m], ens_ref.at[m], in_sems.at[4 + m]) for m in range(MEMBERS)
    ]
    for copy in fetches + members:
        copy.start()
    for copy in fetches:
        copy.wait()
    margin_ref, owner_ref, patch_ref, letkf_ref = landed
    lane24 = iota((24, ELEMENTS), 1)
    block_of = (lane24 // 128) * 8 + lane24 % 8
    pick_block = iota((24, ELEMENTS), 0) == block_of
    expanded = dot(margin_ref[...], one_hot(pick_block))
    row = iota((256, ELEMENTS), 0)
    lane = iota((256, ELEMENTS), 1)
    fits = (row // 128 == (lane % 16) // 8) & (row % 8 == (lane % 128) // 16)
    expanded = jnp.where(fits, expanded, 0.0).astype(BF)
    fold = one_hot((iota((ELEMENTS, 256), 1) % 128) // 8 == iota((ELEMENTS, 256), 0) % 16)
    spread = dot(fold, expanded)
    er = iota((ELEMENTS, ELEMENTS), 0)
    el = iota((ELEMENTS, ELEMENTS), 1)
    spread = jnp.where(er // 16 == (el // 128) * 8 + el % 8, spread, 0.0)
    sums = jnp.sum(spread, axis=0, keepdims=True)
    spread = spread.astype(BF)
    spread_ref[...] = spread
    leaving = [pltpu.make_async_copy(spread_ref, spread_hbm, out_sems.at[8])]
    leaving[0].start()
    high = sums.astype(BF).astype(F32)
    low = sums - high

    dest = owner_ref[...] * 8 + patch_ref[...] - 256
    dest = dest.astype(F32).astype(BF)
    place = dot(dest, one_hot(pick_block))
    lane2 = iota((2, ELEMENTS), 1)
    place = jnp.sum(jnp.where((lane2 % 16) // 8 == iota((2, ELEMENTS), 0), place, 0.0), axis=0, keepdims=True)

    own = mem_ref[0] * MEMBERS
    pick_own = one_hot((iota((16, 40), 1) == own + iota((16, 40), 0)) & (iota((16, 40), 0) < MEMBERS))
    mine = dot_nt(pick_own, letkf_ref[...].astype(BF)).astype(BF)
    lane40 = iota((40, ELEMENTS), 1)
    weights = dot(mine, one_hot(iota((40, ELEMENTS), 0) == (lane40 // 128) * 16 + lane40 % 16))
    sides = [place, high, low] + [weights[n : n + 1] for n in range(MEMBERS)] + [jnp.zeros_like(low)] * 2
    spare = iota((16, ELEMENTS), 0) == 15

    for m in range(MEMBERS):
        members[m].wait()
        for j in range(3):
            rows = slice(m * CHANNELS, (m + 1) * CHANNELS)
            wide_ref[j, rows, :] = ens_ref[m, :, 128 * j : 128 * j + 128].astype(F32)
    for group in range(8):
        if group % 2 == 0:
            tiles = [
                jnp.concatenate([wide_ref[j, pl.ds(start, 16, 16), :] for j in range(3)], axis=1)
                for near in (group, group + 1)
                for start in places(near)
            ]
            product = dot(jnp.concatenate(tiles, axis=0).astype(BF), spread)
        pieces = product[160 * (group % 2) : 160 * (group % 2) + 160]
        pieces = jnp.concatenate(
            [jnp.where(spare, sides[k], pieces[16 * k : 16 * k + 16]) for k in range(10)], axis=0
        )
        firsts = [pieces[0:128, 128 * h : 128 * h + 128].astype(BF).T.reshape(8, ROWS, 128) for h in range(THIRDS)]
        rest = [pieces[128:160, 128 * h : 128 * h + 128] for h in range(THIRDS)]
        rest = jnp.concatenate(rest + [jnp.zeros((32, 128), F32)], axis=0)
        pack(out_ref, slice(8 * group, 8 * group + 8), firsts, rest.T.reshape(8, ROWS, 128))
        part = pl.ds(8 * group, 8)
        leaving.append(pltpu.make_async_copy(out_ref.at[part], out_hbm.at[part], out_sems.at[group]))
        leaving[-1].start()
    for copy in leaving:
        copy.wait()


def hits(first):
    place = first[:, 15:16] + 256.0
    lanes = iota((MESH * ROWS, PATCHES), 1).astype(F32)
    return one_hot(lanes == place)


def patch_kernel(got_ref, out_ref):
    every = slice(0, MESH)
    last_t = unpack_last(got_ref, every).reshape(MESH * ROWS, 128).T
    grid = jnp.zeros((160, PATCHES), F32)
    weights = [[None] * THIRDS for _ in range(MEMBERS)]
    for h in range(THIRDS):
        first = unpack(got_ref, every, h).reshape(MESH * ROWS, 128)
        first_t = first.T
        left = jnp.concatenate([first_t, last_t[32 * h : 32 * h + 32]], axis=0).astype(BF)
        grid = grid + dot(left, hits(first))
        for n in range(MEMBERS):
            weights[n][h] = first_t[63 + 16 * n : 64 + 16 * n]
    cover = grid[31:32] + grid[47:48]
    weights = sum(weights, []) + [jnp.zeros((1, MESH * ROWS), F32)]
    weights = jnp.concatenate(weights, axis=0).astype(BF)
    cover = jnp.maximum(cover, 1.0)
    grid = grid / cover
    for q in range(MEM):
        at = slice(64 * q, 64 * q + 64)
        out_ref[q, 0:80, :] = jnp.concatenate([grid[0:80, at], grid[80:160, at]], axis=1).astype(BF)
        out_ref[q, 80:96, :] = weights[:, 128 * q : 128 * q + 128]


def mixing_kernel(got_ref, out_ref, weight_ref, field_ref):
    tile = one_hot(iota((128, 128), 0) // 16 == (iota((128, 128), 1) % 64) // 8)
    lane = iota((ROWS, 128), 1)
    for q in range(MEM):
        wide = got_ref[q, 80:96, :]
        rows = [jnp.where(lane % 16 == r, wide, jnp.zeros_like(wide)) for r in range(ROWS)]
        weight_ref[q] = dot(jnp.concatenate(rows, axis=0), tile)
        field_ref[q] = got_ref[q, 0:80, :].astype(F32)

    def mix(q, carry):
        mixed = [jnp.zeros((16, 128), F32) for _ in range(MEMBERS)]
        for m in range(MEM * MEMBERS):
            row = (m % MEMBERS) * 16
            field = field_ref[m // MEMBERS, row : row + 16, :]
            for n in range(MEMBERS):
                w = (m % 16) * 16 + n * 3 + m // 16
                mixed[n] = mixed[n] + weight_ref[q, w : w + 1, :] * field
        for n in range(MEMBERS):
            out_ref[q, 16 * n : 16 * n + 16, :] = (mixed[n] - field_ref[q, 16 * n : 16 * n + 16, :]).astype(BF)

    for q in range(MEM):
        mix(q, 0)


def expand_kernel(inc_ref, got_ref, out_ref):
    halves = [[], []]
    for q in range(0, MEM, 2):
        even, odd = inc_ref[q].astype(F32), inc_ref[q + 1].astype(F32)
        halves[0].append(jnp.concatenate([even[:, 0:64], odd[:, 0:64]], axis=1))
        halves[1].append(jnp.concatenate([even[:, 64:128], odd[:, 64:128]], axis=1))
    inc = jnp.concatenate([jnp.concatenate(half, axis=1) for half in halves], axis=0)
    first = inc[0:128].T.astype(BF)
    small = inc[128:160]
    last = jnp.zeros((MESH * ROWS, 128), F32)
    every = slice(0, MESH)
    firsts = []
    for h in range(THIRDS):
        pad = [jnp.zeros((32, PATCHES), F32)] * 4
        pad[h] = small
        right = jnp.concatenate([first, jnp.concatenate(pad, axis=0).T.astype(BF)], axis=1)
        back = dot(hits(unpack(got_ref, every, h).reshape(MESH * ROWS, 128)), right)
        firsts.append(back[:, 0:128].reshape(MESH, ROWS, 128))
        last = last + back[:, 128:256]
    pack(out_ref, every, firsts, last.reshape(MESH, ROWS, 128))


def final_kernel(back_ref, ens_ref, spread_ref, out_hbm, wide_ref, out_ref, sems):
    spread = spread_ref[...]
    area = dot_nt(jnp.ones((16, ELEMENTS), BF), spread)[0:1]
    scale = 1.0 / area
    lefts = []
    for group in range(8):
        at = slice(8 * group, 8 * group + 8)
        first = jnp.concatenate([unpack(back_ref, at, h).reshape(128, 128).astype(BF).T for h in range(THIRDS)], axis=1)
        last = unpack_last(back_ref, at).reshape(128, 128).T
        last = jnp.concatenate([last[32 * h : 32 * h + 32] for h in range(THIRDS)], axis=1)
        lefts.append(jnp.concatenate([first, last.astype(BF)], axis=0))
    corrections = [
        dot_nt(jnp.concatenate(lefts[k : k + 2], axis=0), spread) * scale for k in range(0, 8, 2)
    ]
    copies = []
    for m in range(MEMBERS):
        for j in range(3):
            lanes = slice(128 * j, 128 * j + 128)
            for group in range(8):
                for parity in range(2):
                    row = 160 * (group % 2) + 80 * parity + 16 * m
                    rows = pl.ds(m * CHANNELS + 2 * group + parity, 15, 16)
                    wide_ref[j, rows, :] = corrections[group // 2][row : row + 15, lanes]
            rows = slice(m * CHANNELS, (m + 1) * CHANNELS)
            out_ref[m, :, lanes] = (ens_ref[m, :, lanes].astype(F32) + wide_ref[j, rows, :]).astype(BF)
        copies.append(pltpu.make_async_copy(out_ref.at[m], out_hbm.at[m], sems.at[m]))
        copies[-1].start()
    for copy in copies:
        copy.wait()


def vmem():
    return pl.BlockSpec(memory_space=pltpu.VMEM)


def hbm():
    return pl.BlockSpec(memory_space=pltpu.HBM)


def call(kernel, outs, ins, scratch=(), limit=VMEM_BYTES, place=vmem):
    return pl.pallas_call(
        kernel,
        out_shape=[jax.ShapeDtypeStruct(s, d) for s, d in outs],
        in_specs=ins,
        out_specs=[place() for _ in outs],
        scratch_shapes=list(scratch),
        compiler_params=pltpu.CompilerParams(vmem_limit_bytes=limit),
    )


def shards(ensemble, ovl_owner, ovl_patch, ovl_weight, letkf_weight):
    margin = ovl_weight.transpose(1, 2, 3, 0).reshape(256, 24)
    mem = lax.axis_index("mem").astype(jnp.int32).reshape(1)
    send, spread = call(
        source_kernel,
        [((MESH, QUARTERS, WIDTH), BF), ((ELEMENTS, ELEMENTS), BF)],
        [pl.BlockSpec(memory_space=pltpu.SMEM)] + [hbm()] * 5,
        [
            pltpu.VMEM((MEMBERS, CHANNELS, ELEMENTS), BF),
            pltpu.VMEM((256, 24), BF),
            pltpu.VMEM((2, 24), jnp.int32),
            pltpu.VMEM((2, 24), jnp.int32),
            pltpu.VMEM((MEM * MEMBERS, MEM * MEMBERS), F32),
            pltpu.VMEM((3, WIDE_ROWS, 128), F32),
            pltpu.VMEM((MESH, QUARTERS, WIDTH), BF),
            pltpu.VMEM((ELEMENTS, ELEMENTS), BF),
            pltpu.SemaphoreType.DMA((9,)),
            pltpu.SemaphoreType.DMA((9,)),
        ],
        SOURCE_VMEM_BYTES,
        hbm,
    )(mem, ensemble, margin, ovl_owner.T, ovl_patch.T, letkf_weight[0])
    got = lax.all_to_all(send, "mesh", split_axis=0, concat_axis=0, tiled=True)
    (fields,) = call(patch_kernel, [((MEM, 96, 128), BF)], [vmem()])(got)
    fields = lax.all_to_all(fields, "mem", split_axis=0, concat_axis=0, tiled=True)
    (mixed,) = call(
        mixing_kernel,
        [((MEM, 80, 128), BF)],
        [vmem()],
        [pltpu.VMEM((MEM, 256, 128), F32), pltpu.VMEM((MEM, 80, 128), F32)],
    )(fields)
    mixed = lax.all_to_all(mixed, "mem", split_axis=0, concat_axis=0, tiled=True)
    (back,) = call(expand_kernel, [((MESH, QUARTERS, WIDTH), BF)], [vmem()] * 2)(mixed, got)
    returned = lax.all_to_all(back, "mesh", split_axis=0, concat_axis=0, tiled=True)
    (analysis,) = call(
        final_kernel,
        [((MEMBERS, CHANNELS, ELEMENTS), BF)],
        [vmem()] * 3,
        [
            pltpu.VMEM((3, WIDE_ROWS, 128), F32),
            pltpu.VMEM((MEMBERS, CHANNELS, ELEMENTS), BF),
            pltpu.SemaphoreType.DMA((MEMBERS,)),
        ],
        place=hbm,
    )(returned, ensemble, spread)
    return analysis


def solution(mesh):
    in_specs = (
        P("mem", None, "mesh"),
        P("mesh", None),
        P("mesh", None),
        P("mesh", None, None, None),
        P("mesh", None, None),
    )
    out_specs = P("mem", None, "mesh")
    return jax.shard_map(shards, mesh=mesh, in_specs=in_specs, out_specs=out_specs, check_vma=False)
```

```python
import jax
import jax.numpy as jnp
from jax import lax
from jax.experimental import pallas as pl
from jax.experimental.pallas import tpu as pltpu
from jax.sharding import PartitionSpec as P

MESH = 64
MEM = 8
MEMBERS = 5
CHANNELS = 240
ELEMENTS = 384
CELLS = 8
PATCHES = 512
ROWS = 16
THIRDS = 3
QUARTERS = 4
WIDTH = 1920
WIDE_ROWS = 1216
BF = jnp.bfloat16
F32 = jnp.float32
VMEM_BYTES = 40 * 1024 * 1024
SOURCE_VMEM_BYTES = 60 * 1024 * 1024


def iota(shape, dim):
    return lax.broadcasted_iota(jnp.int32, shape, dim)


def dot(a, b):
    return jnp.dot(a, b, preferred_element_type=F32)


def dot_nt(a, b):
    return lax.dot_general(a, b, (((1,), (1,)), ((), ())), preferred_element_type=F32)


def one_hot(mask):
    return jnp.where(mask, 1.0, 0.0).astype(BF)


def turn(value, shift):
    return pltpu.roll(value, shift, 2)


def pack(out_ref, at, firsts, last):
    for h in range(THIRDS):
        block = firsts[h]
        for a in range(QUARTERS):
            lanes = slice(128 * (3 * a + h), 128 * (3 * a + h) + 128)
            out_ref[at, :, lanes] = block[:, 4 * a : 4 * a + 4, :].astype(BF)
    n = last.shape[0]
    front = iota((n, 4, 128), 2) < 96
    for i in range(THIRDS):
        tail = turn(last, 96 - 32 * i)[:, 12:16, :]
        lanes = slice(128 * (12 + i), 128 * (12 + i) + 128)
        out_ref[at, :, lanes] = jnp.where(front, last[:, 4 * i : 4 * i + 4, :], tail).astype(BF)


def unpack(ref, at, h):
    parts = []
    for a in range(QUARTERS):
        lanes = slice(128 * (3 * a + h), 128 * (3 * a + h) + 128)
        parts.append(ref[at, :, lanes].astype(F32))
    return jnp.concatenate(parts, axis=1)


def unpack_last(ref, at):
    tiles = [ref[at, :, 128 * (12 + i) : 128 * (12 + i) + 128].astype(F32) for i in range(THIRDS)]
    lane = iota(tiles[0].shape, 2) // 32
    tail = turn(tiles[0], 32)
    for h in range(1, THIRDS):
        tail = jnp.where(lane == h, turn(tiles[h], 32 * h + 32), tail)
    return jnp.concatenate(tiles + [tail], axis=1)


def places(group):
    return [m * CHANNELS + 2 * group + parity for parity in range(2) for m in range(MEMBERS)]


def source_kernel(mem_ref, *refs):
    ens_hbm, small, (out_hbm, spread_hbm), landed = refs[0], refs[1:5], refs[5:7], refs[8:12]
    ens_ref, wide_ref, out_ref, spread_ref, in_sems, out_sems = refs[7], *refs[12:17]
    fetches = [pltpu.make_async_copy(a, b, in_sems.at[k]) for k, (a, b) in enumerate(zip(small, landed))]
    members = [
        pltpu.make_async_copy(ens_hbm.at[m], ens_ref.at[m], in_sems.at[4 + m]) for m in range(MEMBERS)
    ]
    for copy in fetches + members:
        copy.start()
    for copy in fetches:
        copy.wait()
    margin_ref, owner_ref, patch_ref, letkf_ref = landed
    lane24 = iota((24, ELEMENTS), 1)
    block_of = (lane24 // 128) * 8 + lane24 % 8
    pick_block = iota((24, ELEMENTS), 0) == block_of
    expanded = dot(margin_ref[...], one_hot(pick_block))
    row = iota((256, ELEMENTS), 0)
    lane = iota((256, ELEMENTS), 1)
    fits = (row // 128 == (lane % 16) // 8) & (row % 8 == (lane % 128) // 16)
    expanded = jnp.where(fits, expanded, 0.0).astype(BF)
    fold = one_hot((iota((ELEMENTS, 256), 1) % 128) // 8 == iota((ELEMENTS, 256), 0) % 16)
    spread = dot(fold, expanded)
    er = iota((ELEMENTS, ELEMENTS), 0)
    el = iota((ELEMENTS, ELEMENTS), 1)
    spread = jnp.where(er // 16 == (el // 128) * 8 + el % 8, spread, 0.0)
    sums = jnp.sum(spread, axis=0, keepdims=True)
    spread = spread.astype(BF)
    spread_ref[...] = spread
    leaving = [pltpu.make_async_copy(spread_ref, spread_hbm, out_sems.at[8])]
    leaving[0].start()
    high = sums.astype(BF).astype(F32)
    low = sums - high

    dest = owner_ref[...] * 8 + patch_ref[...] - 256
    dest = dest.astype(F32).astype(BF)
    place = dot(dest, one_hot(pick_block))
    lane2 = iota((2, ELEMENTS), 1)
    place = jnp.sum(jnp.where((lane2 % 16) // 8 == iota((2, ELEMENTS), 0), place, 0.0), axis=0, keepdims=True)

    own = mem_ref[0] * MEMBERS
    pick_own = one_hot((iota((16, 40), 1) == own + iota((16, 40), 0)) & (iota((16, 40), 0) < MEMBERS))
    mine = dot_nt(pick_own, letkf_ref[...].astype(BF)).astype(BF)
    lane40 = iota((40, ELEMENTS), 1)
    weights = dot(mine, one_hot(iota((40, ELEMENTS), 0) == (lane40 // 128) * 16 + lane40 % 16))
    sides = [place, high, low] + [weights[n : n + 1] for n in range(MEMBERS)] + [jnp.zeros_like(low)] * 2
    spare = iota((16, ELEMENTS), 0) == 15

    for m in range(MEMBERS):
        members[m].wait()
        for j in range(3):
            rows = slice(m * CHANNELS, (m + 1) * CHANNELS)
            wide_ref[j, rows, :] = ens_ref[m, :, 128 * j : 128 * j + 128].astype(F32)
    for group in range(8):
        if group % 2 == 0:
            tiles = [
                jnp.concatenate([wide_ref[j, pl.ds(start, 16, 16), :] for j in range(3)], axis=1)
                for near in (group, group + 1)
                for start in places(near)
            ]
            product = dot(jnp.concatenate(tiles, axis=0).astype(BF), spread)
        pieces = product[160 * (group % 2) : 160 * (group % 2) + 160]
        pieces = jnp.concatenate(
            [jnp.where(spare, sides[k], pieces[16 * k : 16 * k + 16]) for k in range(10)], axis=0
        )
        firsts = [pieces[0:128, 128 * h : 128 * h + 128].astype(BF).T.reshape(8, ROWS, 128) for h in range(THIRDS)]
        rest = [pieces[128:160, 128 * h : 128 * h + 128] for h in range(THIRDS)]
        rest = jnp.concatenate(rest + [jnp.zeros((32, 128), F32)], axis=0)
        pack(out_ref, slice(8 * group, 8 * group + 8), firsts, rest.T.reshape(8, ROWS, 128))
        part = pl.ds(8 * group, 8)
        leaving.append(pltpu.make_async_copy(out_ref.at[part], out_hbm.at[part], out_sems.at[group]))
        leaving[-1].start()
    for copy in leaving:
        copy.wait()


def hits(first):
    place = first[:, 15:16] + 256.0
    lanes = iota((MESH * ROWS, PATCHES), 1).astype(F32)
    return one_hot(lanes == place)


def patch_kernel(got_ref, out_ref):
    every = slice(0, MESH)
    last_t = unpack_last(got_ref, every).reshape(MESH * ROWS, 128).astype(BF).T
    grid = jnp.zeros((160, PATCHES), F32)
    weights = [[None] * THIRDS for _ in range(MEMBERS)]
    for h in range(THIRDS):
        first = unpack(got_ref, every, h).reshape(MESH * ROWS, 128)
        first_t = first.astype(BF).T
        left = jnp.concatenate([first_t, last_t[32 * h : 32 * h + 32]], axis=0)
        grid = grid + dot(left, hits(first))
        for n in range(MEMBERS):
            weights[n][h] = first_t[63 + 16 * n : 64 + 16 * n].astype(F32)
    cover = grid[31:32] + grid[47:48]
    weights = sum(weights, []) + [jnp.zeros((1, MESH * ROWS), F32)]
    weights = jnp.concatenate(weights, axis=0).astype(BF)
    cover = jnp.maximum(cover, 1.0)
    grid = grid / cover
    for q in range(MEM):
        at = slice(64 * q, 64 * q + 64)
        out_ref[q, 0:80, :] = jnp.concatenate([grid[0:80, at], grid[80:160, at]], axis=1).astype(BF)
        out_ref[q, 80:96, :] = weights[:, 128 * q : 128 * q + 128]


def mixing_kernel(got_ref, out_ref, weight_ref, field_ref):
    tile = one_hot(iota((128, 128), 0) // 16 == (iota((128, 128), 1) % 64) // 8)
    lane = iota((ROWS, 128), 1)
    for q in range(MEM):
        wide = got_ref[q, 80:96, :]
        rows = [jnp.where(lane % 16 == r, wide, jnp.zeros_like(wide)) for r in range(ROWS)]
        weight_ref[q] = dot(jnp.concatenate(rows, axis=0), tile)
        field_ref[q] = got_ref[q, 0:80, :].astype(F32)

    def mix(q, carry):
        mixed = [jnp.zeros((16, 128), F32) for _ in range(MEMBERS)]
        for m in range(MEM * MEMBERS):
            row = (m % MEMBERS) * 16
            field = field_ref[m // MEMBERS, row : row + 16, :]
            for n in range(MEMBERS):
                w = (m % 16) * 16 + n * 3 + m // 16
                mixed[n] = mixed[n] + weight_ref[q, w : w + 1, :] * field
        for n in range(MEMBERS):
            out_ref[q, 16 * n : 16 * n + 16, :] = (mixed[n] - field_ref[q, 16 * n : 16 * n + 16, :]).astype(BF)

    for q in range(MEM):
        mix(q, 0)


def expand_kernel(inc_ref, got_ref, out_ref):
    halves = [[], []]
    for q in range(0, MEM, 2):
        even, odd = inc_ref[q].astype(F32), inc_ref[q + 1].astype(F32)
        halves[0].append(jnp.concatenate([even[:, 0:64], odd[:, 0:64]], axis=1))
        halves[1].append(jnp.concatenate([even[:, 64:128], odd[:, 64:128]], axis=1))
    inc = jnp.concatenate([jnp.concatenate(half, axis=1) for half in halves], axis=0)
    first = inc[0:128].astype(BF).T
    small = inc[128:160]
    last = jnp.zeros((MESH * ROWS, 128), F32)
    every = slice(0, MESH)
    firsts = []
    for h in range(THIRDS):
        pad = [jnp.zeros((32, PATCHES), F32)] * 4
        pad[h] = small
        right = jnp.concatenate([first, jnp.concatenate(pad, axis=0).astype(BF).T], axis=1)
        back = dot(hits(unpack(got_ref, every, h).reshape(MESH * ROWS, 128)), right)
        firsts.append(back[:, 0:128].reshape(MESH, ROWS, 128))
        last = last + back[:, 128:256]
    pack(out_ref, every, firsts, last.reshape(MESH, ROWS, 128))


def final_kernel(back_ref, ens_ref, spread_ref, out_hbm, wide_ref, out_ref, sems):
    spread = spread_ref[...]
    area = dot_nt(jnp.ones((16, ELEMENTS), BF), spread)[0:1]
    scale = 1.0 / area
    lefts = []
    for group in range(8):
        at = slice(8 * group, 8 * group + 8)
        first = jnp.concatenate([unpack(back_ref, at, h).reshape(128, 128).astype(BF).T for h in range(THIRDS)], axis=1)
        last = unpack_last(back_ref, at).reshape(128, 128).T
        last = jnp.concatenate([last[32 * h : 32 * h + 32] for h in range(THIRDS)], axis=1)
        lefts.append(jnp.concatenate([first, last.astype(BF)], axis=0))
    corrections = [
        dot_nt(jnp.concatenate(lefts[k : k + 2], axis=0), spread) * scale for k in range(0, 8, 2)
    ]
    copies = []
    for m in range(MEMBERS):
        for j in range(3):
            lanes = slice(128 * j, 128 * j + 128)
            for group in range(8):
                for parity in range(2):
                    row = 160 * (group % 2) + 80 * parity + 16 * m
                    rows = pl.ds(m * CHANNELS + 2 * group + parity, 15, 16)
                    wide_ref[j, rows, :] = corrections[group // 2][row : row + 15, lanes]
            rows = slice(m * CHANNELS, (m + 1) * CHANNELS)
            out_ref[m, :, lanes] = (ens_ref[m, :, lanes].astype(F32) + wide_ref[j, rows, :]).astype(BF)
        copies.append(pltpu.make_async_copy(out_ref.at[m], out_hbm.at[m], sems.at[m]))
        copies[-1].start()
    for copy in copies:
        copy.wait()


def vmem():
    return pl.BlockSpec(memory_space=pltpu.VMEM)


def hbm():
    return pl.BlockSpec(memory_space=pltpu.HBM)


def call(kernel, outs, ins, scratch=(), limit=VMEM_BYTES, place=vmem):
    return pl.pallas_call(
        kernel,
        out_shape=[jax.ShapeDtypeStruct(s, d) for s, d in outs],
        in_specs=ins,
        out_specs=[place() for _ in outs],
        scratch_shapes=list(scratch),
        compiler_params=pltpu.CompilerParams(vmem_limit_bytes=limit),
    )


def shards(ensemble, ovl_owner, ovl_patch, ovl_weight, letkf_weight):
    margin = ovl_weight.transpose(1, 2, 3, 0).reshape(256, 24)
    mem = lax.axis_index("mem").astype(jnp.int32).reshape(1)
    send, spread = call(
        source_kernel,
        [((MESH, QUARTERS, WIDTH), BF), ((ELEMENTS, ELEMENTS), BF)],
        [pl.BlockSpec(memory_space=pltpu.SMEM)] + [hbm()] * 5,
        [
            pltpu.VMEM((MEMBERS, CHANNELS, ELEMENTS), BF),
            pltpu.VMEM((256, 24), BF),
            pltpu.VMEM((2, 24), jnp.int32),
            pltpu.VMEM((2, 24), jnp.int32),
            pltpu.VMEM((MEM * MEMBERS, MEM * MEMBERS), F32),
            pltpu.VMEM((3, WIDE_ROWS, 128), F32),
            pltpu.VMEM((MESH, QUARTERS, WIDTH), BF),
            pltpu.VMEM((ELEMENTS, ELEMENTS), BF),
            pltpu.SemaphoreType.DMA((9,)),
            pltpu.SemaphoreType.DMA((9,)),
        ],
        SOURCE_VMEM_BYTES,
        hbm,
    )(mem, ensemble, margin, ovl_owner.T, ovl_patch.T, letkf_weight[0])
    got = lax.all_to_all(send, "mesh", split_axis=0, concat_axis=0, tiled=True)
    (fields,) = call(patch_kernel, [((MEM, 96, 128), BF)], [vmem()])(got)
    fields = lax.all_to_all(fields, "mem", split_axis=0, concat_axis=0, tiled=True)
    (mixed,) = call(
        mixing_kernel,
        [((MEM, 80, 128), BF)],
        [vmem()],
        [pltpu.VMEM((MEM, 256, 128), F32), pltpu.VMEM((MEM, 80, 128), F32)],
    )(fields)
    mixed = lax.all_to_all(mixed, "mem", split_axis=0, concat_axis=0, tiled=True)
    (back,) = call(expand_kernel, [((MESH, QUARTERS, WIDTH), BF)], [vmem()] * 2)(mixed, got)
    returned = lax.all_to_all(back, "mesh", split_axis=0, concat_axis=0, tiled=True)
    (analysis,) = call(
        final_kernel,
        [((MEMBERS, CHANNELS, ELEMENTS), BF)],
        [vmem()] * 3,
        [
            pltpu.VMEM((3, WIDE_ROWS, 128), F32),
            pltpu.VMEM((MEMBERS, CHANNELS, ELEMENTS), BF),
            pltpu.SemaphoreType.DMA((MEMBERS,)),
        ],
        place=hbm,
    )(returned, ensemble, spread)
    return analysis


def solution(mesh):
    in_specs = (
        P("mem", None, "mesh"),
        P("mesh", None),
        P("mesh", None),
        P("mesh", None, None, None),
        P("mesh", None, None),
    )
    out_specs = P("mem", None, "mesh")
    return jax.shard_map(shards, mesh=mesh, in_specs=in_specs, out_specs=out_specs, check_vma=False)
```
